256 devices in a mesh: leaf: 4 (over y), row: 8 (over x, core), col: 8 (over z).
Axes of the slice: x: 4, y: 4, z: 8, core: 2. Of those that a mesh axis runs over, the one named last changes fastest.
Arguments:
- child_source: float32 [4, 4096, 384], P('leaf', 'col'), may hold values from -6 to 6
- middle_source: float32 [4, 4096, 384], P('leaf', 'col'), may hold values from -6 to 6
- root_source: float32 [16384, 384], P(('leaf', 'col')), may hold values from -6 to 6
- child_inverse: float32 [4, 4096, 4096], P('leaf', 'row', 'col'), may hold values from -0.09375 to 0.09375
- child_update: float32 [4, 2048, 4096], P('leaf', 'col', 'row'), may hold values from -0.09375 to 0.09375
- middle_inverse: float32 [4, 8192, 4096], P('leaf', 'row', 'col'), may hold values from -0.0625 to 0.0625
- middle_update: float32 [4, 2048, 8192], P('leaf', 'col', 'row'), may hold values from -0.0625 to 0.0625
- root_inverse: float32 [16384, 16384], P('row', ('leaf', 'col')), may hold values from -0.046875 to 0.046875
- child_diagmask: int32 [4, 32, 32], P('leaf', 'row', 'col'), may hold values 0 or 1
- child_updmask: int32 [4, 16, 32], P('leaf', 'col', 'row'), may hold values 0 or 1
- middle_diagmask: int32 [4, 64, 32], P('leaf', 'row', 'col'), may hold values 0 or 1
- middle_updmask: int32 [4, 16, 64], P('leaf', 'col', 'row'), may hold values 0 or 1
- root_diagmask: int32 [128, 128], P('row', ('leaf', 'col')), may hold values 0 or 1
- child_rowmap: int32 [4, 2048], replicated, may hold values from 0 to 8191
- middle_rowmap: int32 [2, 4096], replicated, may hold values from 0 to 16383
Outputs:
- child_solution: float32 [4, 4096, 384], P('leaf', 'row', 'col')
- middle_solution: float32 [4, 8192, 192], P('leaf', 'row', 'col')
- root_solution: float32 [16384, 384], P('row', 'col')
The draws below stay inside these ranges and needn't reach their ends.
All inputs are finite; a program needn't handle non-finite values. No bound on the sum of `child_diagmask` or of `child_updmask` or of `middle_diagmask` or of `middle_updmask` or of `root_diagmask` on one device may be relied on, other than what follows from the above.
Results may differ from the reference program's by a relative error of at most 0.0001.
Values sent between devices are 32-bit elements; how exact they have to be, the bound alone decides.
A program may use at most 128 MiB of HBM per device.

```python
import jax
import jax.numpy as jnp
from jax import lax

BLK = 128
P0 = 4096
U0 = 2048
P1 = 8192
U1 = 4096
P2 = 16384
NRHS = 384


def with_ends(entries, own_key, low, high):
    spot = [jax.random.randint(jax.random.fold_in(own_key, axis), (), 0, length) for axis, length in enumerate(entries.shape)]
    main_axis = entries.shape.index(max(entries.shape))
    next_to = spot[:main_axis] + [(spot[main_axis] + 1) % entries.shape[main_axis]] + spot[main_axis + 1:]
    return entries.at[tuple(spot)].set(low).at[tuple(next_to)].set(high)


def steps_of(key, dims, pieces, least, largest):
    factor_of = 1.0
    for dim, parts in pieces:
        draws = jax.random.uniform(jax.random.fold_in(jax.random.fold_in(key, 6), dim), (parts,), jnp.float32, least / len(pieces), largest / len(pieces))
        factor_of = factor_of * jnp.repeat(jnp.exp(draws), dims[dim] // parts).reshape((-1,) + (1,) * (len(dims) - 1 - dim))
    return factor_of


def bell_draw(rng, extent, width, most, cuts=(), held_as=jnp.bfloat16):
    entries = jax.random.normal(rng, extent, jnp.float32) * width
    if len(cuts) > 0:
        entries = steps_of(rng, extent, cuts, -0.22, 0.18) * entries
    return jnp.clip(entries, min=-most, max=most).astype(held_as)


def setup_inputs(seed: int = 0) -> dict:
    arg_keys = jax.random.split(jax.random.key(seed), 16)
    return {
        "child_source": bell_draw(arg_keys[0], (4, P0, NRHS), 1.0, 6.0, ((0, 4), (1, 8)), jnp.float32),
        "middle_source": bell_draw(arg_keys[1], (4, P1 // 2, NRHS), 1.0, 6.0, ((0, 4), (1, 8)), jnp.float32),
        "root_source": bell_draw(arg_keys[2], (P2, NRHS), 1.0, 6.0, ((0, 32),), jnp.float32),
        "child_inverse": bell_draw(arg_keys[3], (4, P0, P0), P0 ** -0.5, 0.09375, ((0, 4), (1, 8), (2, 8)), jnp.float32),
        "child_update": bell_draw(arg_keys[4], (4, U0, P0), P0 ** -0.5, 0.09375, ((0, 4), (1, 8), (2, 8)), jnp.float32),
        "middle_inverse": bell_draw(arg_keys[5], (4, P1, P1 // 2), P1 ** -0.5, 0.0625, ((0, 4), (1, 8), (2, 8)), jnp.float32),
        "middle_update": bell_draw(arg_keys[6], (4, U1 // 2, P1), P1 ** -0.5, 0.0625, ((0, 4), (1, 8), (2, 8)), jnp.float32),
        "root_inverse": bell_draw(arg_keys[7], (P2, P2), P2 ** -0.5, 0.046875, ((0, 8), (1, 32)), jnp.float32),
        "child_diagmask": with_ends((jax.random.randint(arg_keys[8], (4, P0 // BLK, P0 // BLK), 0, 2) < 1).astype(jnp.int32), jax.random.fold_in(arg_keys[8], 1), 0, 1),
        "child_updmask": with_ends((jax.random.randint(arg_keys[9], (4, U0 // BLK, P0 // BLK), 0, 2) < 1).astype(jnp.int32), jax.random.fold_in(arg_keys[9], 1), 0, 1),
        "middle_diagmask": with_ends((jax.random.randint(arg_keys[10], (4, P1 // BLK, P1 // (2 * BLK)), 0, 2) < 1).astype(jnp.int32), jax.random.fold_in(arg_keys[10], 1), 0, 1),
        "middle_updmask": with_ends((jax.random.randint(arg_keys[11], (4, U1 // (2 * BLK), P1 // BLK), 0, 2) < 1).astype(jnp.int32), jax.random.fold_in(arg_keys[11], 1), 0, 1),
        "root_diagmask": with_ends((jax.random.randint(arg_keys[12], (P2 // BLK, P2 // BLK), 0, 2) < 1).astype(jnp.int32), jax.random.fold_in(arg_keys[12], 1), 0, 1),
        "child_rowmap": with_ends(jax.random.randint(arg_keys[13], (4, U0), 0, P1), jax.random.fold_in(arg_keys[13], 1), 0, P1 - 1).astype(jnp.int32),
        "middle_rowmap": with_ends(jax.random.randint(arg_keys[14], (2, U1), 0, P2), jax.random.fold_in(arg_keys[14], 1), 0, P2 - 1).astype(jnp.int32),
    }


def expand(blocks):
    return jnp.repeat(jnp.repeat(blocks, BLK, axis=0), BLK, axis=1)


def keep_lower(pattern):
    rows_count, cols_count = pattern.shape
    row_ids = jnp.arange(rows_count)[:, None]
    col_ids = jnp.arange(cols_count)[None, :]
    keep = (row_ids == col_ids) | ((row_ids > col_ids) & (pattern == 1))
    return expand(keep.astype(jnp.float32))


def masked_product(panel, keep, vector):
    return jnp.dot(panel * keep, vector, precision=lax.Precision.HIGHEST, preferred_element_type=jnp.float32)


def reference(child_source, middle_source, root_source, child_inverse, child_update, middle_inverse, middle_update, root_inverse, child_diagmask, child_updmask, middle_diagmask, middle_updmask, root_diagmask, child_rowmap, middle_rowmap):
    child_values = []
    child_lifts = []
    for child in range(4):
        solved = masked_product(child_inverse[child], keep_lower(child_diagmask[child]), child_source[child])
        child_values.append(solved)
        child_lifts.append(masked_product(child_update[child], expand(child_updmask[child].astype(jnp.float32)), solved))
    middle_values = []
    middle_lifts = []
    for middle in range(2):
        assembled = jnp.concatenate([middle_source[2 * middle], middle_source[2 * middle + 1]], axis=0)
        for half in range(2):
            assembled = assembled.at[child_rowmap[2 * middle + half]].add(child_lifts[2 * middle + half])
        inverse = jnp.concatenate([middle_inverse[2 * middle], middle_inverse[2 * middle + 1]], axis=1)
        pattern = jnp.concatenate([middle_diagmask[2 * middle], middle_diagmask[2 * middle + 1]], axis=1)
        solved = masked_product(inverse, keep_lower(pattern), assembled)
        middle_values.append(solved[:, : NRHS // 2])
        middle_values.append(solved[:, NRHS // 2:])
        update = jnp.concatenate([middle_update[2 * middle], middle_update[2 * middle + 1]], axis=0)
        upattern = jnp.concatenate([middle_updmask[2 * middle], middle_updmask[2 * middle + 1]], axis=0)
        middle_lifts.append(masked_product(update, expand(upattern.astype(jnp.float32)), solved))
    assembled = root_source
    for middle in range(2):
        assembled = assembled.at[middle_rowmap[middle]].add(middle_lifts[middle])
    root_solution = masked_product(root_inverse, keep_lower(root_diagmask), assembled)
    return jnp.stack(child_values), jnp.stack(middle_values), root_solution
```

```python
import functools
from types import SimpleNamespace

import jax
import jax.numpy as jnp
from jax import lax
from jax.experimental import pallas as pl
from jax.experimental.pallas import tpu as pltpu
from jax.sharding import PartitionSpec as P

BLK = 128
BATCHES = 3
COPIES = 256
TILE = 256
MESH = pl.DeviceIdType.MESH
F32 = jnp.float32
BF16 = jnp.bfloat16
NT = (((1,), (1,)), ((), ()))


def run(streams, filler=None):
    live = list(streams)
    while live:
        for stream in list(live):
            if next(stream, StopIteration) is StopIteration:
                live.remove(stream)
        if filler is not None:
            filler.step()


class Filler:
    def __init__(self):
        self.tasks = []

    def add(self, name, pieces):
        self.tasks.append((name, pieces))

    def step(self):
        while self.tasks:
            name, pieces = self.tasks[0]
            if next(pieces, StopIteration) is StopIteration:
                self.tasks.pop(0)
            else:
                return

    def need(self, name):
        while any(task[0] is name for task in self.tasks):
            self.step()


class Links:
    def __init__(self, send_sems, recv_sems):
        self.send_sems = send_sems
        self.recv_sems = recv_sems
        self.count = 0
        self.sent = []

    def send(self, source, landing, target):
        index = self.count
        self.count += 1
        copy = pltpu.make_async_remote_copy(
            src_ref=source,
            dst_ref=landing,
            send_sem=self.send_sems.at[index],
            recv_sem=self.recv_sems.at[index],
            device_id=target,
            device_id_type=MESH,
        )
        copy.start()
        self.sent.append(copy)
        return copy

    def close(self):
        for copy in self.sent:
            copy.wait_send()


class Ring:
    def __init__(self, index, length, device):
        self.index = index
        self.length = length
        self.device = device

    def at(self, offset):
        return lax.rem(self.index + offset + 2 * self.length, self.length)


def ring_reduce_scatter(links, ring, longer, part, landing):
    far = ring.length // 2
    reach = {longer: far, -longer: far - 1}
    before = {}
    for step in range(far + 1):
        if step > 0:
            yield
        for way in (longer, -longer):
            hops = reach[way] - step
            if hops < 0:
                continue
            term = part(ring.at(way * hops))
            if step > 0:
                before[way].wait_recv()
                term[...] = term[...] + landing(way, step - 1)[...]
            if hops > 0:
                before[way] = links.send(term, landing(way, step), ring.device(ring.at(way)))


def ring_all_gather(links, ring, longer, part, arrived=None):
    far = ring.length // 2
    reach = {longer: far, -longer: far - 1}
    before = {}
    for step in range(far + 1):
        if step > 0:
            yield
        new = [ring.index] if step == 0 else []
        for way in (longer, -longer):
            if step > reach[way]:
                continue
            chunk = ring.at(-way * step)
            if step > 0:
                before[way].wait_recv()
                new.append(chunk)
            if step < reach[way]:
                before[way] = links.send(part(chunk), part(chunk), ring.device(ring.at(way)))
        if arrived is not None:
            for chunk in new:
                arrived(chunk)


def split(value):
    high = value.astype(BF16)
    return high, (value - high.astype(F32)).astype(BF16)


def product(left, panel_high, panel_low, out, depth, shape):
    count = left.shape[0] // 2

    def tile(j, carry):
        rows = pl.ds(pl.multiple_of(j * TILE, TILE), TILE)
        both = lax.dot_general(left[:, :depth], panel_high[rows, :], NT, preferred_element_type=F32)
        last = lax.dot_general(
            left[:count, :depth], panel_low[rows, :], NT, preferred_element_type=F32
        )
        out(j)[...] = (both[:count] + both[count:] + last).reshape(shape)
        return carry

    lax.fori_loop(0, panel_high.shape[0] // TILE, tile, 0)


def kernel(sizes, names, *refs):
    ref = SimpleNamespace(**dict(zip(names, refs)))
    n_leaf, n_row, n_col, p0, p1, p2, nrhs = sizes
    n_x = n_row // 2
    leaf, row, col = lax.axis_index("leaf"), lax.axis_index("row"), lax.axis_index("col")
    half, couple = lax.rem(leaf, 2), lax.div(leaf, 2)
    x, core = lax.div(row, 2), lax.rem(row, 2)
    ring_y = Ring(leaf, n_leaf, lambda i: {"leaf": i})
    ring_z = Ring(col, n_col, lambda i: {"col": i})
    ring_x = Ring(x, n_x, lambda i: {"row": i * 2 + core})
    pair = {"leaf": couple * 2 + 1 - half}
    twin = {"row": x * 2 + 1 - core}
    links = Links(ref.send_sems, ref.recv_sems)
    width = nrhs // BATCHES
    share, cshare, mshare = width // n_row, width // n_col, width // 2 // n_col
    groups = width // mshare

    loads = {}
    for index, (source, landing) in enumerate(
        (
            (ref.child_source.at[0], ref.v_child_source),
            (ref.child_inverse.at[0], ref.v_child_inverse),
            (ref.child_update.at[0], ref.v_child_update),
            (ref.middle_source.at[0], ref.v_middle_source),
            (ref.middle_inverse.at[0], ref.v_middle_inverse),
            (ref.middle_update.at[0], ref.v_middle_update),
            (ref.root_source, ref.v_root_source),
            (ref.root_inverse, ref.v_root_inverse),
        )
    ):
        loads[id(landing)] = pltpu.make_async_copy(source, landing, ref.load_sems.at[index])
        loads[id(landing)].start()

    barrier = pltpu.get_barrier_semaphore()
    friends = [twin]
    for ring in (ring_x, ring_y, ring_z):
        friends += [ring.device(ring.at(1)), ring.device(ring.at(-1))]
    for friend in friends:
        pl.semaphore_signal(barrier, inc=1, device_id=friend, device_id_type=MESH)

    def prepare(panel, high, low, mask, first_row, first_col, pieces):
        blocks, across = panel.shape[0] // BLK, panel.shape[1] // BLK
        loads[id(panel)].wait()

        def body(i, carry):
            rows = pl.ds(pl.multiple_of(i * BLK, BLK), BLK)
            for j in range(across):
                kept = mask(i, j) == 1
                if first_row is not None:
                    down, right = first_row + i, first_col + j
                    kept = (down == right) | ((down > right) & kept)
                columns = slice(j * BLK, (j + 1) * BLK)
                block = panel[rows, columns] * kept.astype(F32)
                top, rest = split(block)
                high[rows, columns] = top
                low[rows, columns] = rest
            return carry

        for piece in range(pieces):
            lax.fori_loop(blocks * piece // pieces, blocks * (piece + 1) // pieces, body, 0)
            yield

    def flip(source, flipped):
        loads[id(source)].wait()
        for part in range(source.shape[0] // 256):
            rows = slice(part * 256, (part + 1) * 256)
            flipped[:, :, :, rows] = source[rows, :].T.reshape(groups, BATCHES, mshare, 256)
            yield

    def one_hot(out, rowmap, first, pieces):
        count = out.shape[0]
        place = lax.broadcasted_iota(jnp.int32, out.shape[1:], 0) + first

        def body(k, carry):
            out[k] = (rowmap(k) == place).astype(F32).astype(BF16)
            return carry

        for piece in range(pieces):
            lax.fori_loop(count * piece // pieces, count * (piece + 1) // pieces, body, 0)
            yield

    def child_map(k):
        columns = pl.ds(pl.multiple_of(lax.rem(k, n_col) * TILE, TILE), TILE)
        return ref.child_rowmap[pl.ds(2 * couple + lax.div(k, n_col), 1), columns]

    def middle_map(k):
        owner = lax.div(k, n_col)
        start = (lax.rem(owner, 2) * n_col + lax.rem(k, n_col)) * TILE
        columns = pl.ds(pl.multiple_of(start, TILE), TILE)
        return ref.middle_rowmap[pl.ds(lax.div(owner, 2), 1), columns]

    middle_first = (half * n_col + col) * (p1 // 2 // n_col)
    root_first = (leaf * n_col + col) * (p2 // n_leaf // n_col)
    filler = Filler()
    filler.add(ref.child_update,
        prepare(ref.v_child_update, ref.h_child_update, ref.l_child_update, lambda i, j: ref.child_updmask[0, i, j], None, None, 1),
    )
    filler.add(ref.hot_middle, one_hot(ref.hot_middle, child_map, middle_first, 4))
    filler.add(ref.middle_source, flip(ref.v_middle_source, ref.t_middle_source))
    filler.add(ref.middle_inverse,
        prepare(ref.v_middle_inverse, ref.h_middle_inverse, ref.l_middle_inverse,
            lambda i, j: ref.middle_diagmask[0, i, j],
            row * (p1 // n_row // BLK),
            lax.div(middle_first, BLK),
            4,
        ),
    )
    filler.add(ref.middle_update,
        prepare(ref.v_middle_update, ref.h_middle_update, ref.l_middle_update, lambda i, j: ref.middle_updmask[0, i, j], None, None, 2),
    )
    filler.add(ref.root_source, flip(ref.v_root_source, ref.t_root_source))
    filler.add(ref.hot_root, one_hot(ref.hot_root, middle_map, root_first, 8))
    filler.add(ref.root_inverse,
        prepare(ref.v_root_inverse, ref.h_root_inverse, ref.l_root_inverse,
            lambda i, j: ref.root_diagmask[i, j],
            row * (p2 // n_row // BLK),
            lax.div(root_first, BLK),
            8,
        ),
    )

    for _ in prepare(ref.v_child_inverse, ref.h_child_inverse, ref.l_child_inverse,
        lambda i, j: ref.child_diagmask[0, i, j],
        row * (p0 // n_row // BLK),
        col * (p0 // n_col // BLK),
        1,
    ):
        pass
    for _ in flip(ref.v_child_source, ref.t_child_source):
        pass

    def chain(b):
        longer = 1 if b == 1 else -1
        left = ref.left.at[b]

        def fill_left(value, columns):
            high, low = split(value)
            left[:width, columns] = high
            left[width:, columns] = low

        def lift_reduce(lift, twin_land, land):
            copy = links.send(lift.at[:, 1 - core], twin_land, twin)
            yield
            copy.wait_recv()
            lift[:, core] = lift[:, core] + twin_land[...]
            yield from ring_reduce_scatter(
                links,
                ring_x,
                longer,
                lambda d: lift.at[d, core],
                lambda way, step: land.at[(way + 1) // 2, step],
            )

        def row_gather(buffer):
            copies = []

            def arrived(d):
                copies.append(links.send(buffer.at[d, core], buffer.at[d, core], twin))

            yield from ring_all_gather(
                links, ring_x, longer, lambda d: buffer.at[d, core], arrived
            )
            yield
            for copy in copies:
                copy.wait_recv()

        def add_block(total, block, hot):
            high = block.astype(BF16).astype(F32)
            both = jnp.concatenate([high, block - high], axis=0).astype(BF16)
            total[...] += lax.dot_general(both, hot, NT, preferred_element_type=F32)

        depth = p0 // n_col
        fill_left(ref.t_child_source[:, b].reshape(width, depth), slice(0, depth))
        terms = ref.child_terms.at[b]
        product(
            left,
            ref.h_child_inverse,
            ref.l_child_inverse,
            lambda j: terms.at[j],
            depth,
            (n_col, cshare, TILE),
        )
        if b == 0:
            pl.semaphore_wait(barrier, len(friends))
        yield from ring_reduce_scatter(
            links,
            ring_z,
            longer,
            lambda d: terms.at[:, d],
            lambda way, step: ref.child_land.at[b, (way + 1) // 2, step],
        )
        value = ref.child_value.at[b]
        value[:, col] = terms[:, col]
        ref.child_out[:, :, b] = terms[:, col].reshape(p0 // n_row // TILE, 2, mshare, TILE)
        yield from ring_all_gather(links, ring_z, longer, lambda d: value.at[:, d])

        filler.need(ref.child_update)
        for j in range(p0 // n_row // TILE):
            fill_left(value[j].reshape(width, TILE), slice(j * TILE, (j + 1) * TILE))
        lift = ref.child_lift.at[b]
        product(
            left,
            ref.h_child_update,
            ref.l_child_update,
            lambda j: lift,
            p0 // n_row,
            (n_x, 2, share, TILE),
        )
        yield from lift_reduce(lift, ref.child_twin.at[b], ref.child_lift_land.at[b])

        got = ref.child_lifts.at[b]
        got[half, col] = lift[x, core]
        copy = links.send(got.at[half, col], got.at[half, col], pair)
        filler.need(ref.hot_middle)
        total = ref.middle_total.at[b]
        total[...] = jnp.zeros_like(total)
        yield
        copy.wait_recv()

        def child_arrived(d):
            for which in range(2):
                add_block(total, got[which, d], ref.hot_middle[which * n_col + d])

        yield from ring_all_gather(links, ring_z, longer, lambda d: got.at[:, d], child_arrived)
        filler.need(ref.middle_source)
        rhs = ref.middle_rhs.at[b]
        source = ref.t_middle_source[pl.ds(2 * row, 2), b].reshape(share, -1)
        rhs[x, core] = source + total[:share] + total[share:]
        yield from row_gather(rhs)

        filler.need(ref.middle_inverse)
        depth = p1 // 2 // n_col
        fill_left(rhs[...].reshape(width, depth), slice(0, depth))
        mid = ref.middle_terms.at[b]
        tiles = p1 // n_row // TILE
        product(
            left,
            ref.h_middle_inverse,
            ref.l_middle_inverse,
            lambda j: mid.at[j],
            depth,
            (2, n_col, mshare, TILE),
        )
        yield from ring_reduce_scatter(
            links,
            ring_z,
            longer,
            lambda d: mid.at[:, :, d],
            lambda way, step: ref.middle_land.at[b, (way + 1) // 2, step],
        )
        copy = links.send(mid.at[:, 1 - half, col], ref.middle_pair.at[b], pair)
        yield
        copy.wait_recv()
        solved = ref.middle_value.at[b]
        summed = mid[:, half, col] + ref.middle_pair[b]
        solved[:, half, col] = summed
        ref.middle_out[:, b] = summed
        copy = links.send(solved.at[:, half, col], solved.at[:, half, col], pair)
        yield
        copy.wait_recv()
        yield from ring_all_gather(links, ring_z, longer, lambda d: solved.at[:, :, d])

        filler.need(ref.middle_update)
        for j in range(tiles):
            fill_left(solved[j].reshape(width, TILE), slice(j * TILE, (j + 1) * TILE))
        lift2 = ref.middle_lift.at[b]
        product(
            left,
            ref.h_middle_update,
            ref.l_middle_update,
            lambda j: lift2,
            p1 // n_row,
            (n_x, 2, share, TILE),
        )
        yield from lift_reduce(lift2, ref.middle_twin.at[b], ref.middle_lift_land.at[b])

        every = ref.middle_lifts.at[b]
        every[leaf, col] = lift2[x, core]
        yield from ring_all_gather(links, ring_y, longer, lambda d: every.at[d, col])
        filler.need(ref.hot_root)
        total2 = ref.root_total.at[b]
        total2[...] = jnp.zeros_like(total2)

        def middle_arrived(d):
            for which in range(n_leaf):
                add_block(total2, every[which, d], ref.hot_root[which * n_col + d])

        yield from ring_all_gather(links, ring_z, longer, lambda d: every.at[:, d], middle_arrived)
        filler.need(ref.root_source)
        rhs2 = ref.root_rhs.at[b]
        source2 = ref.t_root_source[pl.ds(2 * row, 2), b].reshape(share, -1)
        rhs2[x, core] = source2 + total2[:share] + total2[share:]
        yield from row_gather(rhs2)

        filler.need(ref.root_inverse)
        depth = p2 // n_leaf // n_col
        fill_left(rhs2[...].reshape(width, depth), slice(0, depth))
        root = ref.root_terms.at[b]
        each = p2 // n_row // TILE // n_leaf
        product(
            left,
            ref.h_root_inverse,
            ref.l_root_inverse,
            lambda j: root.at[j],
            depth,
            (n_col, cshare, TILE),
        )
        if b == 0:
            yield from ring_reduce_scatter(
                links,
                ring_z,
                longer,
                lambda d: root.at[:, d],
                lambda way, step: ref.root_land_az.at[(way + 1) // 2, step],
            )
            yield from ring_reduce_scatter(
                links,
                ring_y,
                longer,
                lambda d: root.at[pl.ds(d * each, each), col],
                lambda way, step: ref.root_land_ay.at[(way + 1) // 2, step],
            )
        else:
            yield from ring_reduce_scatter(
                links,
                ring_y,
                longer,
                lambda d: root.at[pl.ds(d * each, each)],
                lambda way, step: ref.root_land_by.at[b - 1, (way + 1) // 2, step],
            )
            yield from ring_reduce_scatter(
                links,
                ring_z,
                longer,
                lambda d: root.at[pl.ds(leaf * each, each), d],
                lambda way, step: ref.root_land_bz.at[b - 1, (way + 1) // 2, step],
            )
        final = ref.root_out
        mine = root[pl.ds(leaf * each, each), col]
        final[pl.ds(leaf * each, each), :, b] = mine.reshape(each, 2, mshare, TILE)
        yield from ring_all_gather(
            links, ring_y, longer, lambda d: final.at[pl.ds(d * each, each), :, b]
        )

    run([chain(b) for b in range(BATCHES)], filler)
    assert links.count <= COPIES
    links.close()


def local(
    n_leaf,
    n_row,
    n_col,
    child_source,
    middle_source,
    root_source,
    child_inverse,
    child_update,
    middle_inverse,
    middle_update,
    root_inverse,
    child_diagmask,
    child_updmask,
    middle_diagmask,
    middle_updmask,
    root_diagmask,
    child_rowmap,
    middle_rowmap,
):
    given = dict(
        child_source=child_source,
        middle_source=middle_source,
        root_source=root_source,
        child_inverse=child_inverse,
        child_update=child_update,
        middle_inverse=middle_inverse,
        middle_update=middle_update,
        root_inverse=root_inverse,
        child_diagmask=child_diagmask,
        child_updmask=child_updmask,
        middle_diagmask=middle_diagmask,
        middle_updmask=middle_updmask,
        root_diagmask=root_diagmask,
        child_rowmap=child_rowmap,
        middle_rowmap=middle_rowmap,
    )
    nrhs = child_source.shape[2]
    p0 = child_inverse.shape[2] * n_col
    p1 = middle_inverse.shape[1] * n_row
    p2 = root_inverse.shape[0] * n_row
    sizes = (n_leaf, n_row, n_col, p0, p1, p2, nrhs)
    n_x = n_row // 2
    width = nrhs // BATCHES
    share, cshare, mshare = width // n_row, width // n_col, width // 2 // n_col
    groups = width // mshare
    reach_z, reach_y, reach_x = n_col // 2, n_leaf // 2, n_x // 2
    t0, t1, t2 = (p // n_row // TILE for p in (p0, p1, p2))
    scratch = dict(
        v_child_inverse=pltpu.VMEM(child_inverse.shape[-2:], F32),
        h_child_inverse=pltpu.VMEM(child_inverse.shape[-2:], BF16),
        l_child_inverse=pltpu.VMEM(child_inverse.shape[-2:], BF16),
        v_child_update=pltpu.VMEM(child_update.shape[-2:], F32),
        h_child_update=pltpu.VMEM(child_update.shape[-2:], BF16),
        l_child_update=pltpu.VMEM(child_update.shape[-2:], BF16),
        v_middle_inverse=pltpu.VMEM(middle_inverse.shape[-2:], F32),
        h_middle_inverse=pltpu.VMEM(middle_inverse.shape[-2:], BF16),
        l_middle_inverse=pltpu.VMEM(middle_inverse.shape[-2:], BF16),
        v_middle_update=pltpu.VMEM(middle_update.shape[-2:], F32),
        h_middle_update=pltpu.VMEM(middle_update.shape[-2:], BF16),
        l_middle_update=pltpu.VMEM(middle_update.shape[-2:], BF16),
        v_root_inverse=pltpu.VMEM(root_inverse.shape[-2:], F32),
        h_root_inverse=pltpu.VMEM(root_inverse.shape[-2:], BF16),
        l_root_inverse=pltpu.VMEM(root_inverse.shape[-2:], BF16),
        v_child_source=pltpu.VMEM(child_source.shape[-2:], F32),
        t_child_source=pltpu.VMEM((groups, BATCHES, mshare, child_source.shape[-2]), F32),
        v_middle_source=pltpu.VMEM(middle_source.shape[-2:], F32),
        t_middle_source=pltpu.VMEM((groups, BATCHES, mshare, middle_source.shape[-2]), F32),
        v_root_source=pltpu.VMEM(root_source.shape[-2:], F32),
        t_root_source=pltpu.VMEM((groups, BATCHES, mshare, root_source.shape[-2]), F32),
    )
    d1, d2 = p1 // 2 // n_col, p2 // n_leaf // n_col
    depth = max(p0 // n_col, p0 // n_row, d1, p1 // n_row, d2)
    scratch.update(left=pltpu.VMEM((BATCHES, 2 * width, depth), BF16))
    scratch.update(hot_middle=pltpu.VMEM((2 * n_col, d1, TILE), BF16))
    scratch.update(hot_root=pltpu.VMEM((n_leaf * n_col, d2, TILE), BF16))
    shapes = dict(
        child_terms=(BATCHES, t0, n_col, cshare, TILE),
        child_land=(BATCHES, 2, reach_z, t0, cshare, TILE),
        child_value=(BATCHES, t0, n_col, cshare, TILE),
        child_lift=(BATCHES, n_x, 2, share, TILE),
        child_twin=(BATCHES, n_x, share, TILE),
        child_lift_land=(BATCHES, 2, reach_x, share, TILE),
        child_lifts=(BATCHES, 2, n_col, share, TILE),
        middle_total=(BATCHES, 2 * share, d1),
        middle_rhs=(BATCHES, n_x, 2, share, d1),
        middle_terms=(BATCHES, t1, 2, n_col, mshare, TILE),
        middle_land=(BATCHES, 2, reach_z, t1, 2, mshare, TILE),
        middle_pair=(BATCHES, t1, mshare, TILE),
        middle_value=(BATCHES, t1, 2, n_col, mshare, TILE),
        middle_lift=(BATCHES, n_x, 2, share, TILE),
        middle_twin=(BATCHES, n_x, share, TILE),
        middle_lift_land=(BATCHES, 2, reach_x, share, TILE),
        middle_lifts=(BATCHES, n_leaf, n_col, share, TILE),
        root_total=(BATCHES, 2 * share, d2),
        root_rhs=(BATCHES, n_x, 2, share, d2),
        root_terms=(BATCHES, t2, n_col, cshare, TILE),
        root_land_az=(2, reach_z, t2, cshare, TILE),
        root_land_ay=(2, reach_y, t2 // n_leaf, cshare, TILE),
        root_land_by=(BATCHES - 1, 2, reach_y, t2 // n_leaf, n_col, cshare, TILE),
        root_land_bz=(BATCHES - 1, 2, reach_z, t2 // n_leaf, cshare, TILE),
    )
    for name, shape in shapes.items():
        scratch[name] = pltpu.VMEM(shape, F32)
    scratch.update(send_sems=pltpu.SemaphoreType.DMA((COPIES,)))
    scratch.update(recv_sems=pltpu.SemaphoreType.DMA((COPIES,)))
    scratch.update(load_sems=pltpu.SemaphoreType.DMA((8,)))
    outs = dict(
        child_out=(t0, 2, BATCHES, mshare, TILE),
        middle_out=(t1, BATCHES, mshare, TILE),
        root_out=(t2, 2, BATCHES, mshare, TILE),
    )
    vmem = pl.BlockSpec(memory_space=pltpu.VMEM)
    smem = pl.BlockSpec(memory_space=pltpu.SMEM)
    whole = pl.BlockSpec(memory_space=pl.ANY)
    child, middle, root = pl.pallas_call(
        functools.partial(kernel, sizes, tuple(given) + tuple(outs) + tuple(scratch)),
        out_shape=[jax.ShapeDtypeStruct(shape, F32) for shape in outs.values()],
        in_specs=[whole] * 8 + [smem] * 5 + [vmem] * 2,
        out_specs=[vmem] * 3,
        scratch_shapes=list(scratch.values()),
        compiler_params=pltpu.CompilerParams(
            collective_id=0, has_side_effects=True, vmem_limit_bytes=60 * 2**20
        ),
    )(*given.values())
    return tuple(
        blocks.reshape(*lead, blocks.shape[0], -1, TILE)
        .swapaxes(-1, -2)
        .reshape(*lead, blocks.shape[0] * TILE, -1)
        for blocks, lead in ((child, (1,)), (middle, (1,)), (root, ()))
    )


def solution(mesh):
    placed = (
        P("leaf", "col", None),
        P("leaf", "col", None),
        P(("leaf", "col"), None),
        P("leaf", "row", "col"),
        P("leaf", "col", "row"),
        P("leaf", "row", "col"),
        P("leaf", "col", "row"),
        P("row", ("leaf", "col")),
        P("leaf", "row", "col"),
        P("leaf", "col", "row"),
        P("leaf", "row", "col"),
        P("leaf", "col", "row"),
        P("row", ("leaf", "col")),
        P(),
        P(),
    )
    counts = (mesh.shape["leaf"], mesh.shape["row"], mesh.shape["col"])
    return jax.shard_map(
        functools.partial(local, *counts),
        mesh=mesh,
        in_specs=placed,
        out_specs=(P("leaf", "row", "col"), P("leaf", "row", "col"), P("row", "col")),
        check_vma=False,
    )
```

```python
import functools
from types import SimpleNamespace

import jax
import jax.numpy as jnp
from jax import lax
from jax.experimental import pallas as pl
from jax.experimental.pallas import tpu as pltpu
from jax.sharding import PartitionSpec as P

BLK = 128
BATCHES = 3
COPIES = 256
TILE = 256
MESH = pl.DeviceIdType.MESH
F32 = jnp.float32
BF16 = jnp.bfloat16
NT = (((1,), (1,)), ((), ()))


def run(streams, filler=None):
    live = list(streams)
    while live:
        for stream in list(live):
            if next(stream, StopIteration) is StopIteration:
                live.remove(stream)
        if filler is not None:
            filler.step()


class Filler:
    def __init__(self):
        self.tasks = []

    def add(self, name, pieces):
        self.tasks.append((name, pieces))

    def step(self):
        while self.tasks:
            name, pieces = self.tasks[0]
            if next(pieces, StopIteration) is StopIteration:
                self.tasks.pop(0)
            else:
                return

    def need(self, name):
        while any(task[0] is name for task in self.tasks):
            self.step()


class Links:
    def __init__(self, send_sems, recv_sems):
        self.send_sems = send_sems
        self.recv_sems = recv_sems
        self.count = 0
        self.sent = []

    def send(self, source, landing, target):
        index = self.count
        self.count += 1
        copy = pltpu.make_async_remote_copy(
            src_ref=source,
            dst_ref=landing,
            send_sem=self.send_sems.at[index],
            recv_sem=self.recv_sems.at[index],
            device_id=target,
            device_id_type=MESH,
        )
        copy.start()
        self.sent.append(copy)
        return copy

    def close(self):
        for copy in self.sent:
            copy.wait_send()


class Ring:
    def __init__(self, index, length, device):
        self.index = index
        self.length = length
        self.device = device

    def at(self, offset):
        return lax.rem(self.index + offset + 2 * self.length, self.length)


def ring_reduce_scatter(links, ring, longer, part, landing):
    far = ring.length // 2
    reach = {longer: far, -longer: far - 1}
    before = {}
    for step in range(far + 1):
        if step > 0:
            yield
        for way in (longer, -longer):
            hops = reach[way] - step
            if hops < 0:
                continue
            term = part(ring.at(way * hops))
            if step > 0:
                before[way].wait_recv()
                term[...] = term[...] + landing(way, step - 1)[...]
            if hops > 0:
                before[way] = links.send(term, landing(way, step), ring.device(ring.at(way)))


def fold_reduce_scatter(links, ring, longer, part, landing):
    before = {}
    for step in range(4):
        if step > 0:
            yield
        for way in (longer, -longer):
            term = part(ring.at(way * (3 - step)))
            if step > 0:
                before[way].wait_recv()
                term[...] = term[...] + landing((way + 1) // 2 * 3 + step - 1)[...]
            if step == 1 and way == longer:
                opposite.wait_recv()
                term[...] = term[...] + landing(6)[...]
            if step < 3:
                before[way] = links.send(
                    term, landing((way + 1) // 2 * 3 + step), ring.device(ring.at(way))
                )
        if step == 0:
            opposite = links.send(
                part(ring.at(4)), landing(6), ring.device(ring.at(2 * longer))
            )


def fold_all_gather(links, ring, longer, part, arrived=None):
    before = {}
    for step in range(4):
        if step > 0:
            yield
        new = [ring.index] if step == 0 else []
        for way in (longer, -longer):
            chunk = ring.at(-way * step)
            if step > 0:
                before[way].wait_recv()
                new.append(chunk)
            if step < 3:
                before[way] = links.send(part(chunk), part(chunk), ring.device(ring.at(way)))
        if step == 2:
            chunk = ring.at(-longer * 2)
            opposite = links.send(part(chunk), part(chunk), ring.device(ring.at(2 * longer)))
        if arrived is not None:
            for chunk in new:
                arrived(chunk)
    opposite.wait_recv()
    if arrived is not None:
        arrived(ring.at(4))


def direct_reduce_scatter(links, ring, part, landing):
    copies = []
    for slot, offset in enumerate((2, 1, -1)):
        target = ring.at(offset)
        copies.append(links.send(part(target), landing(slot), ring.device(target)))
    yield
    term = part(ring.index)
    for slot in (1, 2, 0):
        copies[slot].wait_recv()
        term[...] = term[...] + landing(slot)[...]


def direct_all_gather(links, ring, part, arrived=None):
    own = part(ring.index)
    copies = []
    for offset in (2, 1, -1):
        copies.append(links.send(own, own, ring.device(ring.at(offset))))
    if arrived is not None:
        arrived(ring.index)
    yield
    for copy, offset in zip(copies[1:] + copies[:1], (1, -1, 2)):
        copy.wait_recv()
        if arrived is not None:
            arrived(ring.at(-offset))


def split(value):
    high = value.astype(BF16)
    return high, (value - high.astype(F32)).astype(BF16)


def product(left, panel_high, panel_low, out, depth, shape):
    count = left.shape[0] // 2

    def tile(j, carry):
        rows = pl.ds(pl.multiple_of(j * TILE, TILE), TILE)
        both = lax.dot_general(left[:, :depth], panel_high[rows, :], NT, preferred_element_type=F32)
        last = lax.dot_general(
            left[:count, :depth], panel_low[rows, :], NT, preferred_element_type=F32
        )
        out(j)[...] = (both[:count] + both[count:] + last).reshape(shape)
        return carry

    lax.fori_loop(0, panel_high.shape[0] // TILE, tile, 0)


def kernel(sizes, names, *refs):
    ref = SimpleNamespace(**dict(zip(names, refs)))
    n_leaf, n_row, n_col, p0, p1, p2, nrhs = sizes
    n_x = n_row // 2
    leaf, row, col = lax.axis_index("leaf"), lax.axis_index("row"), lax.axis_index("col")
    half, couple = lax.rem(leaf, 2), lax.div(leaf, 2)
    x, core = lax.div(row, 2), lax.rem(row, 2)
    ring_y = Ring(leaf, n_leaf, lambda i: {"leaf": i})
    ring_z = Ring(col, n_col, lambda i: {"col": i})
    ring_x = Ring(x, n_x, lambda i: {"row": i * 2 + core})
    pair = {"leaf": couple * 2 + 1 - half}
    twin = {"row": x * 2 + 1 - core}
    links = Links(ref.send_sems, ref.recv_sems)
    width = nrhs // BATCHES
    share, cshare, mshare = width // n_row, width // n_col, width // 2 // n_col
    groups = width // mshare

    loads = {}
    for index, (source, landing) in enumerate(
        (
            (ref.child_source.at[0], ref.v_child_source),
            (ref.child_inverse.at[0], ref.v_child_inverse),
            (ref.child_update.at[0], ref.v_child_update),
            (ref.middle_source.at[0], ref.v_middle_source),
            (ref.middle_inverse.at[0], ref.v_middle_inverse),
            (ref.middle_update.at[0], ref.v_middle_update),
            (ref.root_source, ref.v_root_source),
            (ref.root_inverse, ref.v_root_inverse),
        )
    ):
        loads[id(landing)] = pltpu.make_async_copy(source, landing, ref.load_sems.at[index])
        loads[id(landing)].start()

    barrier = pltpu.get_barrier_semaphore()
    friends = [twin]
    for ring, offsets in ((ring_x, (1, -1, 2)), (ring_y, (1, -1, 2)), (ring_z, (1, -1, 2, -2))):
        friends += [ring.device(ring.at(offset)) for offset in offsets]
    for friend in friends:
        pl.semaphore_signal(barrier, inc=1, device_id=friend, device_id_type=MESH)

    def prepare(panel, high, low, mask, first_row, first_col, pieces, masked=None):
        blocks, across = panel.shape[0] // BLK, panel.shape[1] // BLK
        loads[id(panel)].wait()

        def body(i, carry):
            rows = pl.ds(pl.multiple_of(i * BLK, BLK), BLK)
            for j in range(across):
                kept = (mask(i, j) == 1).astype(F32)
                if first_row is not None:
                    down, right = first_row + i, first_col + j
                    kept = jnp.where(down == right, 1.0, jnp.where(down > right, kept, 0.0))
                columns = slice(j * BLK, (j + 1) * BLK)
                block = panel[rows, columns] * kept
                if masked is not None:
                    masked[rows, columns] = block
                top, rest = split(block)
                high[rows, columns] = top
                low[rows, columns] = rest
            return carry

        for piece in range(pieces):
            lax.fori_loop(blocks * piece // pieces, blocks * (piece + 1) // pieces, body, 0)
            yield

    def flip(source, flipped):
        loads[id(source)].wait()
        for part in range(source.shape[0] // 256):
            rows = slice(part * 256, (part + 1) * 256)
            flipped[:, :, :, rows] = source[rows, :].T.reshape(groups, BATCHES, mshare, 256)
            yield

    def one_hot(out, rowmap, first, pieces):
        count = out.shape[0]
        place = lax.broadcasted_iota(jnp.int32, out.shape[1:], 0) + first

        def body(k, carry):
            out[k] = (rowmap(k) == place).astype(F32).astype(BF16)
            return carry

        for piece in range(pieces):
            lax.fori_loop(count * piece // pieces, count * (piece + 1) // pieces, body, 0)
            yield

    def child_map(k):
        columns = pl.ds(pl.multiple_of(lax.rem(k, n_col) * TILE, TILE), TILE)
        return ref.child_rowmap[pl.ds(2 * couple + lax.div(k, n_col), 1), columns]

    def middle_map(k):
        owner = lax.div(k, n_col)
        start = (lax.rem(owner, 2) * n_col + lax.rem(k, n_col)) * TILE
        columns = pl.ds(pl.multiple_of(start, TILE), TILE)
        return ref.middle_rowmap[pl.ds(lax.div(owner, 2), 1), columns]

    middle_first = (half * n_col + col) * (p1 // 2 // n_col)
    root_first = (leaf * n_col + col) * (p2 // n_leaf // n_col)
    rows1 = p1 // 4 // n_col
    swap = []

    def share_update():
        here = pl.ds(pl.multiple_of(half * rows1, rows1), rows1)
        yield from prepare(
            ref.v_middle_update,
            ref.h_middle_update.at[here],
            ref.l_middle_update.at[here],
            lambda i, j: ref.middle_updmask[0, pl.ds(i, 1), j : j + 1],
            None,
            None,
            2,
            ref.masked_update,
        )
        swap.append(links.send(ref.masked_update, ref.other_update, pair))

    def split_other():
        swap[0].wait_recv()
        for start in range(0, rows1, BLK):
            there = pl.ds(pl.multiple_of((1 - half) * rows1 + start, BLK), BLK)
            top, rest = split(ref.other_update[start : start + BLK, :])
            ref.h_middle_update[there, :] = top
            ref.l_middle_update[there, :] = rest
            yield

    filler = Filler()
    filler.add(ref.masked_update, share_update())
    filler.add(ref.child_update,
        prepare(ref.v_child_update, ref.h_child_update, ref.l_child_update, lambda i, j: ref.child_updmask[0, pl.ds(i, 1), j : j + 1], None, None, 1),
    )
    filler.add(ref.hot_middle, one_hot(ref.hot_middle, child_map, middle_first, 4))
    filler.add(ref.middle_source, flip(ref.v_middle_source, ref.t_middle_source))
    filler.add(ref.middle_inverse,
        prepare(ref.v_middle_inverse, ref.h_middle_inverse, ref.l_middle_inverse,
            lambda i, j: ref.middle_diagmask[0, pl.ds(i, 1), j : j + 1],
            row * (p1 // n_row // BLK),
            lax.div(middle_first, BLK),
            4,
        ),
    )
    filler.add(ref.middle_update, split_other())
    filler.add(ref.root_source, flip(ref.v_root_source, ref.t_root_source))
    filler.add(ref.hot_root, one_hot(ref.hot_root, middle_map, root_first, 8))
    filler.add(ref.root_inverse,
        prepare(ref.v_root_inverse, ref.h_root_inverse, ref.l_root_inverse,
            lambda i, j: ref.root_diagmask[pl.ds(i, 1), j : j + 1],
            row * (p2 // n_row // BLK),
            lax.div(root_first, BLK),
            8,
        ),
    )

    for _ in prepare(ref.v_child_inverse, ref.h_child_inverse, ref.l_child_inverse,
        lambda i, j: ref.child_diagmask[0, pl.ds(i, 1), j : j + 1],
        row * (p0 // n_row // BLK),
        col * (p0 // n_col // BLK),
        1,
    ):
        pass
    for _ in flip(ref.v_child_source, ref.t_child_source):
        pass

    def chain(b):
        longer = 1 if b == 1 else -1
        left = ref.left.at[b]

        def fill_left(value, columns):
            high, low = split(value)
            left[:width, columns] = high
            left[width:, columns] = low

        def lift_reduce(lift, twin_land, land):
            copy = links.send(lift.at[:, :, 1 - core], twin_land, twin)
            yield
            copy.wait_recv()
            lift[:, :, core] = lift[:, :, core] + twin_land[...]
            yield from direct_reduce_scatter(
                links, ring_x, lambda d: lift.at[:, d, core], lambda slot: land.at[slot]
            )

        def row_gather(buffer):
            copies = []

            def arrived(d):
                copies.append(links.send(buffer.at[d, core], buffer.at[d, core], twin))

            yield from direct_all_gather(links, ring_x, lambda d: buffer.at[d, core], arrived)
            yield
            for copy in copies:
                copy.wait_recv()

        def add_block(total, block, hot):
            high = block.astype(BF16).astype(F32)
            both = jnp.concatenate([high, block - high], axis=0).astype(BF16)
            total[...] += lax.dot_general(both, hot, NT, preferred_element_type=F32)

        depth = p0 // n_col
        fill_left(ref.t_child_source[:, b].reshape(width, depth), slice(0, depth))
        terms = ref.child_terms.at[b]
        product(
            left,
            ref.h_child_inverse,
            ref.l_child_inverse,
            lambda j: terms.at[j],
            depth,
            (n_col, cshare, TILE),
        )
        if b == 0:
            pl.semaphore_wait(barrier, len(friends))
        yield from fold_reduce_scatter(
            links, ring_z, longer, lambda d: terms.at[:, d], lambda slot: ref.child_land.at[b, slot]
        )
        value = ref.child_value.at[b]
        value[:, col] = terms[:, col]
        ref.child_out[:, :, b] = terms[:, col].reshape(p0 // n_row // TILE, 2, mshare, TILE)
        yield from fold_all_gather(links, ring_z, longer, lambda d: value.at[:, d])

        filler.need(ref.child_update)
        for j in range(p0 // n_row // TILE):
            fill_left(value[j].reshape(width, TILE), slice(j * TILE, (j + 1) * TILE))
        lift = ref.child_lift.at[b]
        product(
            left,
            ref.h_child_update,
            ref.l_child_update,
            lambda j: lift.at[j],
            p0 // n_row,
            (n_x, 2, share, TILE),
        )
        yield from lift_reduce(lift, ref.child_twin.at[b], ref.child_lift_land.at[b])

        got = ref.child_lifts.at[b]
        got[half, col] = lift[0, x, core]
        copy = links.send(got.at[half, col], got.at[half, col], pair)
        filler.need(ref.hot_middle)
        total = ref.middle_total.at[b]
        total[...] = jnp.zeros_like(total)
        yield
        copy.wait_recv()

        def child_arrived(d):
            for which in range(2):
                add_block(total, got[which, d], ref.hot_middle[which * n_col + d])

        yield from fold_all_gather(links, ring_z, longer, lambda d: got.at[:, d], child_arrived)
        filler.need(ref.middle_source)
        rhs = ref.middle_rhs.at[b]
        source = ref.t_middle_source[pl.ds(2 * row, 2), b].reshape(share, -1)
        rhs[x, core] = source + total[:share] + total[share:]
        yield from row_gather(rhs)

        filler.need(ref.middle_inverse)
        depth = p1 // 2 // n_col
        fill_left(rhs[...].reshape(width, depth), slice(0, depth))
        mid = ref.middle_terms.at[b]
        tiles = p1 // n_row // TILE
        product(
            left,
            ref.h_middle_inverse,
            ref.l_middle_inverse,
            lambda j: mid.at[j],
            depth,
            (2, n_col, mshare, TILE),
        )
        yield from fold_reduce_scatter(
            links, ring_z, longer, lambda d: mid.at[:, :, d], lambda slot: ref.middle_land.at[b, slot]
        )
        copy = links.send(mid.at[:, 1 - half, col], ref.middle_pair.at[b], pair)
        yield
        copy.wait_recv()
        solved = ref.middle_value.at[b]
        summed = mid[:, half, col] + ref.middle_pair[b]
        solved[:, col] = summed
        ref.middle_out[:, b] = summed
        yield from fold_all_gather(links, ring_z, longer, lambda d: solved.at[:, d])

        filler.need(ref.middle_update)
        narrow = width // 2
        for j in range(tiles):
            high, low = split(solved[j].reshape(narrow, TILE))
            left[:narrow, j * TILE : (j + 1) * TILE] = high
            left[narrow:width, j * TILE : (j + 1) * TILE] = low
        lift2 = ref.middle_lift.at[b]
        product(
            left.at[:width],
            ref.h_middle_update,
            ref.l_middle_update,
            lambda j: lift2.at[j],
            p1 // n_row,
            (n_x, 2, mshare, TILE),
        )
        yield from lift_reduce(lift2, ref.middle_twin.at[b], ref.middle_lift_land.at[b])

        every = ref.middle_lifts.at[b]
        every[leaf, col] = lift2[:, x, core]
        yield from direct_all_gather(links, ring_y, lambda d: every.at[d, col])
        filler.need(ref.hot_root)
        total2 = ref.root_total.at[b]
        total2[...] = jnp.zeros_like(total2)

        def middle_arrived(d):
            for which in range(n_leaf):
                first, part = which // 2 * 2, which % 2
                block = jnp.concatenate([every[first, d, part], every[first + 1, d, part]], axis=0)
                add_block(total2, block, ref.hot_root[which * n_col + d])

        yield from fold_all_gather(links, ring_z, longer, lambda d: every.at[:, d], middle_arrived)
        filler.need(ref.root_source)
        rhs2 = ref.root_rhs.at[b]
        summed2 = total2[:share] + total2[share:]
        for part in range(2):
            source2 = ref.t_root_source[part * n_row + row, b]
            rhs2[x, core, part] = source2 + summed2[part * mshare : (part + 1) * mshare]
        yield from row_gather(rhs2)

        filler.need(ref.root_inverse)
        depth = p2 // n_leaf // n_col
        for part in range(2):
            high, low = split(rhs2[:, :, part].reshape(narrow, depth))
            left[part * narrow : (part + 1) * narrow, :depth] = high
            left[width + part * narrow : width + (part + 1) * narrow, :depth] = low
        root = ref.root_terms.at[b]
        each = p2 // n_row // TILE // n_leaf
        product(
            left,
            ref.h_root_inverse,
            ref.l_root_inverse,
            lambda j: root.at[j],
            depth,
            (n_col, cshare, TILE),
        )
        if b == 0:
            yield from fold_reduce_scatter(
                links, ring_z, longer, lambda d: root.at[:, d], lambda slot: ref.root_land_az.at[slot]
            )
            yield from direct_reduce_scatter(
                links,
                ring_y,
                lambda d: root.at[pl.ds(d * each, each), col],
                lambda slot: ref.root_land_ay.at[slot],
            )
        else:
            yield from ring_reduce_scatter(
                links,
                ring_y,
                longer,
                lambda d: root.at[pl.ds(d * each, each)],
                lambda way, step: ref.root_land_by.at[b - 1, (way + 1) // 2, step],
            )
            yield from fold_reduce_scatter(
                links,
                ring_z,
                longer,
                lambda d: root.at[pl.ds(leaf * each, each), d],
                lambda slot: ref.root_land_bz.at[b - 1, slot],
            )
        final = ref.root_out
        mine = root[pl.ds(leaf * each, each), col]
        final[pl.ds(leaf * each, each), :, b] = mine.reshape(each, 2, mshare, TILE)
        yield from direct_all_gather(
            links, ring_y, lambda d: final.at[pl.ds(d * each, each), :, b]
        )

    run([chain(b) for b in range(BATCHES)], filler)
    assert links.count <= COPIES
    links.close()


def local(
    n_leaf,
    n_row,
    n_col,
    child_source,
    middle_source,
    root_source,
    child_inverse,
    child_update,
    middle_inverse,
    middle_update,
    root_inverse,
    child_diagmask,
    child_updmask,
    middle_diagmask,
    middle_updmask,
    root_diagmask,
    child_rowmap,
    middle_rowmap,
):
    given = dict(
        child_source=child_source,
        middle_source=middle_source,
        root_source=root_source,
        child_inverse=child_inverse,
        child_update=child_update,
        middle_inverse=middle_inverse,
        middle_update=middle_update,
        root_inverse=root_inverse,
        child_diagmask=child_diagmask,
        child_updmask=child_updmask,
        middle_diagmask=middle_diagmask,
        middle_updmask=middle_updmask,
        root_diagmask=root_diagmask,
        child_rowmap=child_rowmap,
        middle_rowmap=middle_rowmap,
    )
    nrhs = child_source.shape[2]
    p0 = child_inverse.shape[2] * n_col
    p1 = middle_inverse.shape[1] * n_row
    p2 = root_inverse.shape[0] * n_row
    sizes = (n_leaf, n_row, n_col, p0, p1, p2, nrhs)
    n_x = n_row // 2
    width = nrhs // BATCHES
    share, cshare, mshare = width // n_row, width // n_col, width // 2 // n_col
    groups = width // mshare
    reach_y = n_leaf // 2
    t0, t1, t2 = (p // n_row // TILE for p in (p0, p1, p2))
    scratch = dict(
        v_child_inverse=pltpu.VMEM(child_inverse.shape[-2:], F32),
        h_child_inverse=pltpu.VMEM(child_inverse.shape[-2:], BF16),
        l_child_inverse=pltpu.VMEM(child_inverse.shape[-2:], BF16),
        v_child_update=pltpu.VMEM(child_update.shape[-2:], F32),
        h_child_update=pltpu.VMEM(child_update.shape[-2:], BF16),
        l_child_update=pltpu.VMEM(child_update.shape[-2:], BF16),
        v_middle_inverse=pltpu.VMEM(middle_inverse.shape[-2:], F32),
        h_middle_inverse=pltpu.VMEM(middle_inverse.shape[-2:], BF16),
        l_middle_inverse=pltpu.VMEM(middle_inverse.shape[-2:], BF16),
        v_middle_update=pltpu.VMEM(middle_update.shape[-2:], F32),
        h_middle_update=pltpu.VMEM((2 * middle_update.shape[-2], middle_update.shape[-1]), BF16),
        l_middle_update=pltpu.VMEM((2 * middle_update.shape[-2], middle_update.shape[-1]), BF16),
        masked_update=pltpu.VMEM(middle_update.shape[-2:], F32),
        other_update=pltpu.VMEM(middle_update.shape[-2:], F32),
        v_root_inverse=pltpu.VMEM(root_inverse.shape[-2:], F32),
        h_root_inverse=pltpu.VMEM(root_inverse.shape[-2:], BF16),
        l_root_inverse=pltpu.VMEM(root_inverse.shape[-2:], BF16),
        v_child_source=pltpu.VMEM(child_source.shape[-2:], F32),
        t_child_source=pltpu.VMEM((groups, BATCHES, mshare, child_source.shape[-2]), F32),
        v_middle_source=pltpu.VMEM(middle_source.shape[-2:], F32),
        t_middle_source=pltpu.VMEM((groups, BATCHES, mshare, middle_source.shape[-2]), F32),
        v_root_source=pltpu.VMEM(root_source.shape[-2:], F32),
        t_root_source=pltpu.VMEM((groups, BATCHES, mshare, root_source.shape[-2]), F32),
    )
    d1, d2 = p1 // 2 // n_col, p2 // n_leaf // n_col
    depth = max(p0 // n_col, p0 // n_row, d1, p1 // n_row, d2)
    scratch.update(left=pltpu.VMEM((BATCHES, 2 * width, depth), BF16))
    scratch.update(hot_middle=pltpu.VMEM((2 * n_col, d1, TILE), BF16))
    scratch.update(hot_root=pltpu.VMEM((n_leaf * n_col, d2, TILE), BF16))
    shapes = dict(
        child_terms=(BATCHES, t0, n_col, cshare, TILE),
        child_land=(BATCHES, 7, t0, cshare, TILE),
        child_value=(BATCHES, t0, n_col, cshare, TILE),
        child_lift=(BATCHES, 1, n_x, 2, share, TILE),
        child_twin=(BATCHES, 1, n_x, share, TILE),
        child_lift_land=(BATCHES, 3, 1, share, TILE),
        child_lifts=(BATCHES, 2, n_col, share, TILE),
        middle_total=(BATCHES, 2 * share, d1),
        middle_rhs=(BATCHES, n_x, 2, share, d1),
        middle_terms=(BATCHES, t1, 2, n_col, mshare, TILE),
        middle_land=(BATCHES, 7, t1, 2, mshare, TILE),
        middle_pair=(BATCHES, t1, mshare, TILE),
        middle_value=(BATCHES, t1, n_col, mshare, TILE),
        middle_lift=(BATCHES, 2, n_x, 2, mshare, TILE),
        middle_twin=(BATCHES, 2, n_x, mshare, TILE),
        middle_lift_land=(BATCHES, 3, 2, mshare, TILE),
        middle_lifts=(BATCHES, n_leaf, n_col, 2, mshare, TILE),
        root_total=(BATCHES, 2 * share, d2),
        root_rhs=(BATCHES, n_x, 2, 2, mshare, d2),
        root_terms=(BATCHES, t2, n_col, cshare, TILE),
        root_land_az=(7, t2, cshare, TILE),
        root_land_ay=(3, t2 // n_leaf, cshare, TILE),
        root_land_by=(BATCHES - 1, 2, reach_y, t2 // n_leaf, n_col, cshare, TILE),
        root_land_bz=(BATCHES - 1, 7, t2 // n_leaf, cshare, TILE),
    )
    for name, shape in shapes.items():
        scratch[name] = pltpu.VMEM(shape, F32)
    scratch.update(send_sems=pltpu.SemaphoreType.DMA((COPIES,)))
    scratch.update(recv_sems=pltpu.SemaphoreType.DMA((COPIES,)))
    scratch.update(load_sems=pltpu.SemaphoreType.DMA((8,)))
    outs = dict(
        child_out=(t0, 2, BATCHES, mshare, TILE),
        middle_out=(t1, BATCHES, mshare, TILE),
        root_out=(t2, 2, BATCHES, mshare, TILE),
    )
    vmem = pl.BlockSpec(memory_space=pltpu.VMEM)
    whole = pl.BlockSpec(memory_space=pl.ANY)
    child, middle, root = pl.pallas_call(
        functools.partial(kernel, sizes, tuple(given) + tuple(outs) + tuple(scratch)),
        out_shape=[jax.ShapeDtypeStruct(shape, F32) for shape in outs.values()],
        in_specs=[whole] * 8 + [vmem] * 7,
        out_specs=[vmem] * 3,
        scratch_shapes=list(scratch.values()),
        compiler_params=pltpu.CompilerParams(
            collective_id=0, has_side_effects=True, vmem_limit_bytes=60 * 2**20
        ),
    )(*given.values())
    return tuple(
        blocks.reshape(*lead, blocks.shape[0], -1, TILE)
        .swapaxes(-1, -2)
        .reshape(*lead, blocks.shape[0] * TILE, -1)
        for blocks, lead in ((child, (1,)), (middle, (1,)), (root, ()))
    )


def solution(mesh):
    placed = (
        P("leaf", "col", None),
        P("leaf", "col", None),
        P(("leaf", "col"), None),
        P("leaf", "row", "col"),
        P("leaf", "col", "row"),
        P("leaf", "row", "col"),
        P("leaf", "col", "row"),
        P("row", ("leaf", "col")),
        P("leaf", "row", "col"),
        P("leaf", "col", "row"),
        P("leaf", "row", "col"),
        P("leaf", "col", "row"),
        P("row", ("leaf", "col")),
        P(),
        P(),
    )
    counts = (mesh.shape["leaf"], mesh.shape["row"], mesh.shape["col"])
    return jax.shard_map(
        functools.partial(local, *counts),
        mesh=mesh,
        in_specs=placed,
        out_specs=(P("leaf", "row", "col"), P("leaf", "row", "col"), P("row", "col")),
        check_vma=False,
    )
```

```python
import functools
from types import SimpleNamespace

import jax
import jax.numpy as jnp
from jax import lax
from jax.experimental import pallas as pl
from jax.experimental.pallas import tpu as pltpu
from jax.sharding import PartitionSpec as P

BLK = 128
BATCHES = 3
COPIES = 320
TILE = 256
MESH = pl.DeviceIdType.MESH
F32 = jnp.float32
BF16 = jnp.bfloat16
NT = (((1,), (1,)), ((), ()))


def run(streams, filler=None):
    live = list(streams)
    while live:
        for stream in list(live):
            if next(stream, StopIteration) is StopIteration:
                live.remove(stream)
        if filler is not None:
            filler.step()


def together(*streams):
    live = list(streams)
    while live:
        for stream in list(live):
            if next(stream, StopIteration) is StopIteration:
                live.remove(stream)
        if live:
            yield


class Filler:
    def __init__(self):
        self.tasks = []

    def add(self, name, pieces):
        self.tasks.append((name, pieces))

    def step(self):
        while self.tasks:
            name, pieces = self.tasks[0]
            if next(pieces, StopIteration) is StopIteration:
                self.tasks.pop(0)
            else:
                return

    def need(self, name):
        while any(task[0] is name for task in self.tasks):
            self.step()


class Links:
    def __init__(self, send_sems, recv_sems):
        self.send_sems = send_sems
        self.recv_sems = recv_sems
        self.count = 0
        self.sent = []

    def send(self, source, landing, target):
        index = self.count
        self.count += 1
        copy = pltpu.make_async_remote_copy(
            src_ref=source,
            dst_ref=landing,
            send_sem=self.send_sems.at[index],
            recv_sem=self.recv_sems.at[index],
            device_id=target,
            device_id_type=MESH,
        )
        copy.start()
        self.sent.append(copy)
        return copy

    def close(self):
        for copy in self.sent:
            copy.wait_send()


class Ring:
    def __init__(self, index, length, device):
        self.index = index
        self.length = length
        self.device = device

    def at(self, offset):
        return lax.rem(self.index + offset + 2 * self.length, self.length)


def ring_reduce_scatter(links, ring, longer, part, landing):
    far = ring.length // 2
    reach = {longer: far, -longer: far - 1}
    before = {}
    for step in range(far + 1):
        if step > 0:
            yield
        for way in (longer, -longer):
            hops = reach[way] - step
            if hops < 0:
                continue
            term = part(ring.at(way * hops))
            if step > 0:
                before[way].wait_recv()
                term[...] = term[...] + landing(way, step - 1)[...]
            if hops > 0:
                before[way] = links.send(term, landing(way, step), ring.device(ring.at(way)))


def fold_reduce_scatter(links, ring, longer, part, landing):
    before = {}
    opposite = links.send(part(ring.at(4)), landing(6), ring.device(ring.at(2 * longer)))
    for step in range(4):
        if step > 0:
            yield
        for way in (longer, -longer):
            term = part(ring.at(way * (3 - step)))
            if step > 0:
                before[way].wait_recv()
                term[...] = term[...] + landing((way + 1) // 2 * 3 + step - 1)[...]
            if step == 1 and way == longer:
                opposite.wait_recv()
                term[...] = term[...] + landing(6)[...]
            if step < 3:
                before[way] = links.send(
                    term, landing((way + 1) // 2 * 3 + step), ring.device(ring.at(way))
                )


def fold_all_gather(links, ring, longer, part, arrived=None):
    before = {}
    for step in range(4):
        if step > 0:
            yield
        new = [ring.index] if step == 0 else []
        for way in (longer, -longer):
            chunk = ring.at(-way * step)
            if step > 0:
                before[way].wait_recv()
                new.append(chunk)
            if step == 2 and way == longer:
                opposite = links.send(part(chunk), part(chunk), ring.device(ring.at(2 * way)))
            if step < 3:
                before[way] = links.send(part(chunk), part(chunk), ring.device(ring.at(way)))
        if arrived is not None:
            for chunk in new:
                arrived(chunk)
    opposite.wait_recv()
    if arrived is not None:
        arrived(ring.at(4))


def direct_reduce_scatter(links, ring, part, landing):
    copies = []
    for slot, offset in enumerate((2, 1, -1)):
        target = ring.at(offset)
        copies.append(links.send(part(target), landing(slot), ring.device(target)))
    yield
    term = part(ring.index)
    for slot in (1, 2, 0):
        copies[slot].wait_recv()
        term[...] = term[...] + landing(slot)[...]


def direct_all_gather(links, ring, part, arrived=None):
    own = part(ring.index)
    copies = []
    for offset in (2, 1, -1):
        copies.append(links.send(own, own, ring.device(ring.at(offset))))
    if arrived is not None:
        arrived(ring.index)
    yield
    for copy, offset in zip(copies[1:] + copies[:1], (1, -1, 2)):
        copy.wait_recv()
        if arrived is not None:
            arrived(ring.at(-offset))


def split(value):
    high = value.astype(BF16)
    return high, (value - high.astype(F32)).astype(BF16)


def product(left, panel_high, panel_low, out, depth, shape):
    count = left.shape[0] // 2

    def tile(j, carry):
        rows = pl.ds(pl.multiple_of(j * TILE, TILE), TILE)
        both = lax.dot_general(left[:, :depth], panel_high[rows, :], NT, preferred_element_type=F32)
        last = lax.dot_general(
            left[:count, :depth], panel_low[rows, :], NT, preferred_element_type=F32
        )
        out(j)[...] = (both[:count] + both[count:] + last).reshape(shape)
        return carry

    lax.fori_loop(0, panel_high.shape[0] // TILE, tile, 0)


def kernel(sizes, names, *refs):
    ref = SimpleNamespace(**dict(zip(names, refs)))
    n_leaf, n_row, n_col, p0, p1, p2, nrhs = sizes
    n_x = n_row // 2
    leaf, row, col = lax.axis_index("leaf"), lax.axis_index("row"), lax.axis_index("col")
    half, couple = lax.rem(leaf, 2), lax.div(leaf, 2)
    x, core = lax.div(row, 2), lax.rem(row, 2)
    ring_y = Ring(leaf, n_leaf, lambda i: {"leaf": i})
    ring_z = Ring(col, n_col, lambda i: {"col": i})
    ring_x = Ring(x, n_x, lambda i: {"row": i * 2 + core})
    pair = {"leaf": couple * 2 + 1 - half}
    twin = {"row": x * 2 + 1 - core}
    links = Links(ref.send_sems, ref.recv_sems)
    width = nrhs // BATCHES
    share, cshare, mshare = width // n_row, width // n_col, width // 2 // n_col
    groups = width // mshare

    loads = {}
    for index, (source, landing) in enumerate(
        (
            (ref.child_source.at[0], ref.v_child_source),
            (ref.child_inverse.at[0], ref.v_child_inverse),
            (ref.child_update.at[0], ref.v_child_update),
            (ref.middle_source.at[0], ref.v_middle_source),
            (ref.middle_inverse.at[0], ref.v_middle_inverse),
            (ref.middle_update.at[0], ref.v_middle_update),
            (ref.root_source, ref.v_root_source),
            (ref.root_inverse, ref.v_root_inverse),
        )
    ):
        loads[id(landing)] = pltpu.make_async_copy(source, landing, ref.load_sems.at[index])
        if index < 2:
            loads[id(landing)].start()

    barrier = pltpu.get_barrier_semaphore()
    friends = [twin]
    for ring, offsets in ((ring_x, (1, -1, 2)), (ring_y, (1, -1, 2)), (ring_z, (1, -1, 2, -2))):
        friends += [ring.device(ring.at(offset)) for offset in offsets]
    friends += [pair | ring_x.device(ring_x.at(offset)) for offset in (1, -1, 2)]
    for friend in friends:
        pl.semaphore_signal(barrier, inc=1, device_id=friend, device_id_type=MESH)

    def prepare(panel, high, low, mask, first_row, first_col, pieces, masked=None, unrolled=False):
        blocks, across = panel.shape[0] // BLK, panel.shape[1] // BLK
        loads[id(panel)].wait()

        def body(i, carry):
            rows = pl.ds(i * BLK if unrolled else pl.multiple_of(i * BLK, BLK), BLK)
            for j in range(across):
                kept = (mask(i, j) == 1).astype(F32)
                if first_row is not None:
                    down, right = first_row + i, first_col + j
                    kept = jnp.where(down == right, 1.0, jnp.where(down > right, kept, 0.0))
                columns = slice(j * BLK, (j + 1) * BLK)
                block = panel[rows, columns] * kept
                if masked is not None:
                    masked[rows, columns] = block
                top, rest = split(block)
                high[rows, columns] = top
                low[rows, columns] = rest
            return carry

        for piece in range(pieces):
            if unrolled:
                for i in range(blocks * piece // pieces, blocks * (piece + 1) // pieces):
                    body(i, 0)
            else:
                lax.fori_loop(blocks * piece // pieces, blocks * (piece + 1) // pieces, body, 0)
            yield

    def flip(source, flipped):
        loads[id(source)].wait()
        for part in range(source.shape[0] // 256):
            rows = slice(part * 256, (part + 1) * 256)
            flipped[:, :, :, rows] = source[rows, :].T.reshape(groups, BATCHES, mshare, 256)
            yield

    def one_hot(out, rowmap, first, pieces):
        count = out.shape[0]
        place = lax.broadcasted_iota(jnp.int32, out.shape[1:], 0) + first

        def body(k, carry):
            out[k] = (rowmap(k) == place).astype(F32).astype(BF16)
            return carry

        for piece in range(pieces):
            lax.fori_loop(count * piece // pieces, count * (piece + 1) // pieces, body, 0)
            yield

    def child_map(k):
        columns = pl.ds(pl.multiple_of(lax.rem(k, n_col) * TILE, TILE), TILE)
        return ref.child_rowmap[pl.ds(2 * couple + lax.div(k, n_col), 1), columns]

    def middle_map(k):
        owner = lax.div(k, n_col)
        start = (lax.rem(owner, 2) * n_col + lax.rem(k, n_col)) * TILE
        columns = pl.ds(pl.multiple_of(start, TILE), TILE)
        return ref.middle_rowmap[pl.ds(lax.div(owner, 2), 1), columns]

    middle_first = (half * n_col + col) * (p1 // 2 // n_col)
    root_first = (leaf * n_col + col) * (p2 // n_leaf // n_col)
    rows1 = p1 // 4 // n_col
    swap = []

    def share_update():
        here = pl.ds(pl.multiple_of(half * rows1, rows1), rows1)
        yield from prepare(
            ref.v_middle_update,
            ref.h_middle_update.at[here],
            ref.l_middle_update.at[here],
            lambda i, j: ref.middle_updmask[0, pl.ds(i, 1), j : j + 1],
            None,
            None,
            2,
            ref.masked_update,
        )
        swap.append(links.send(ref.masked_update, ref.other_update, pair))

    def split_other():
        swap[0].wait_recv()
        for start in range(0, rows1, BLK):
            there = pl.ds(pl.multiple_of((1 - half) * rows1 + start, BLK), BLK)
            top, rest = split(ref.other_update[start : start + BLK, :])
            ref.h_middle_update[there, :] = top
            ref.l_middle_update[there, :] = rest
            yield

    filler = Filler()
    filler.add(ref.masked_update, share_update())
    filler.add(ref.child_update,
        prepare(ref.v_child_update, ref.h_child_update, ref.l_child_update, lambda i, j: ref.child_updmask[0, pl.ds(i, 1), j : j + 1], None, None, 1),
    )
    filler.add(ref.hot_middle, one_hot(ref.hot_middle, child_map, middle_first, 4))
    filler.add(ref.middle_source, flip(ref.v_middle_source, ref.t_middle_source))
    filler.add(ref.middle_inverse,
        prepare(ref.v_middle_inverse, ref.h_middle_inverse, ref.l_middle_inverse,
            lambda i, j: ref.middle_diagmask[0, j : j + 1, i : i + 1],
            row * (p1 // n_row // BLK),
            lax.div(middle_first, BLK),
            4,
            unrolled=True,
        ),
    )
    filler.add(ref.middle_update, split_other())
    filler.add(ref.root_source, flip(ref.v_root_source, ref.t_root_source))
    filler.add(ref.hot_root, one_hot(ref.hot_root, middle_map, root_first, 8))
    filler.add(ref.root_inverse,
        prepare(ref.v_root_inverse, ref.h_root_inverse, ref.l_root_inverse,
            lambda i, j: ref.root_diagmask[j : j + 1, i : i + 1],
            row * (p2 // n_row // BLK),
            lax.div(root_first, BLK),
            8,
            unrolled=True,
        ),
    )

    for _ in prepare(ref.v_child_inverse, ref.h_child_inverse, ref.l_child_inverse,
        lambda i, j: ref.child_diagmask[0, pl.ds(i, 1), j : j + 1],
        row * (p0 // n_row // BLK),
        col * (p0 // n_col // BLK),
        1,
    ):
        pass
    for _ in flip(ref.v_child_source, ref.t_child_source):
        pass
    for load in list(loads.values())[2:]:
        load.start()

    def chain(b):
        longer = 1 if b == 1 else -1
        left = ref.left.at[b]

        def fill_left(value, columns):
            high, low = split(value)
            left[:width, columns] = high
            left[width:, columns] = low

        def lift_reduce(lift, twin_land, land):
            copy = links.send(lift.at[:, :, 1 - core], twin_land, twin)
            yield
            copy.wait_recv()
            lift[:, :, core] = lift[:, :, core] + twin_land[...]
            yield from direct_reduce_scatter(
                links, ring_x, lambda d: lift.at[:, d, core], lambda slot: land.at[slot]
            )

        def row_gather(buffer):
            copies = []

            def arrived(d):
                copies.append(links.send(buffer.at[d, core], buffer.at[d, core], twin))

            yield from direct_all_gather(links, ring_x, lambda d: buffer.at[d, core], arrived)
            yield
            for copy in copies:
                copy.wait_recv()

        def add_block(total, block, hot):
            high = block.astype(BF16).astype(F32)
            both = jnp.concatenate([high, block - high], axis=0).astype(BF16)
            total[...] += lax.dot_general(both, hot, NT, preferred_element_type=F32)

        depth = p0 // n_col
        fill_left(ref.t_child_source[:, b].reshape(width, depth), slice(0, depth))
        terms = ref.child_terms.at[b]
        product(
            left,
            ref.h_child_inverse,
            ref.l_child_inverse,
            lambda j: terms.at[j],
            depth,
            (n_col, cshare, TILE),
        )
        if b == 0:
            pl.semaphore_wait(barrier, len(friends))
        yield from fold_reduce_scatter(
            links, ring_z, longer, lambda d: terms.at[:, d], lambda slot: ref.child_land.at[b, slot]
        )
        value = ref.child_value.at[b]
        value[:, col] = terms[:, col]
        for j in range(p0 // n_row // TILE):
            ref.child_out[:, b, :, j * TILE : (j + 1) * TILE] = terms[j, col].reshape(2, mshare, TILE)
        yield from fold_all_gather(links, ring_z, longer, lambda d: value.at[:, d])

        filler.need(ref.child_update)
        for j in range(p0 // n_row // TILE):
            fill_left(value[j].reshape(width, TILE), slice(j * TILE, (j + 1) * TILE))
        lift = ref.child_lift.at[b]
        product(
            left,
            ref.h_child_update,
            ref.l_child_update,
            lambda j: lift.at[j],
            p0 // n_row,
            (n_x, 2, share, TILE),
        )
        copy = links.send(lift.at[:, :, 1 - core], ref.child_twin.at[b], twin)
        yield
        copy.wait_recv()
        lift[:, :, core] = lift[:, :, core] + ref.child_twin[b]

        land = ref.child_lift_land.at[b]
        copies = []
        for slot, offset in enumerate((2, 1, -1)):
            there = ring_x.at(offset)
            term = lift.at[0, there, core]
            copies.append(links.send(term, land.at[slot], ring_x.device(there)))
            copies.append(links.send(term, land.at[slot + 3], pair | ring_x.device(there)))
        copies.append(links.send(lift.at[0, x, core], land.at[6], pair))
        got = ref.child_lifts.at[b]
        filler.need(ref.hot_middle)
        total = ref.middle_total.at[b]
        total[...] = jnp.zeros_like(total)
        yield
        for copy in copies:
            copy.wait_recv()
        got[half, col] = lift[0, x, core] + land[0] + land[1] + land[2]
        got[1 - half, col] = land[3] + land[4] + land[5] + land[6]

        def child_arrived(d):
            for which in range(2):
                add_block(total, got[which, d], ref.hot_middle[which * n_col + d])

        yield from fold_all_gather(links, ring_z, longer, lambda d: got.at[:, d], child_arrived)
        filler.need(ref.middle_source)
        rhs = ref.middle_rhs.at[b]
        source = ref.t_middle_source[pl.ds(2 * row, 2), b].reshape(share, -1)
        rhs[x, core] = source + total[:share] + total[share:]
        yield from row_gather(rhs)

        filler.need(ref.middle_inverse)
        depth = p1 // 2 // n_col
        fill_left(rhs[...].reshape(width, depth), slice(0, depth))
        mid = ref.middle_terms.at[b]
        tiles = p1 // n_row // TILE
        product(
            left,
            ref.h_middle_inverse,
            ref.l_middle_inverse,
            lambda j: mid.at[j],
            depth,
            (2, n_col, mshare, TILE),
        )
        yield from fold_reduce_scatter(
            links, ring_z, longer, lambda d: mid.at[:, :, d], lambda slot: ref.middle_land.at[b, slot]
        )
        copy = links.send(mid.at[:, 1 - half, col], ref.middle_pair.at[b], pair)
        yield
        copy.wait_recv()
        solved = ref.middle_value.at[b]
        summed = mid[:, half, col] + ref.middle_pair[b]
        solved[:, col] = summed
        for j in range(tiles):
            ref.middle_out[b, :, j * TILE : (j + 1) * TILE] = summed[j]
        yield from fold_all_gather(links, ring_z, longer, lambda d: solved.at[:, d])

        filler.need(ref.middle_update)
        narrow = width // 2
        for j in range(tiles):
            high, low = split(solved[j].reshape(narrow, TILE))
            left[:narrow, j * TILE : (j + 1) * TILE] = high
            left[narrow:width, j * TILE : (j + 1) * TILE] = low
        lift2 = ref.middle_lift.at[b]
        product(
            left.at[:width],
            ref.h_middle_update,
            ref.l_middle_update,
            lambda j: lift2.at[j],
            p1 // n_row,
            (n_x, 2, mshare, TILE),
        )
        yield from lift_reduce(lift2, ref.middle_twin.at[b], ref.middle_lift_land.at[b])

        every = ref.middle_lifts.at[b]
        every[leaf, col] = lift2[:, x, core]
        yield from direct_all_gather(links, ring_y, lambda d: every.at[d, col])
        filler.need(ref.hot_root)
        total2 = ref.root_total.at[b]
        total2[...] = jnp.zeros_like(total2)

        def middle_arrived(d):
            for which in range(n_leaf):
                first, part = which // 2 * 2, which % 2
                block = jnp.concatenate([every[first, d, part], every[first + 1, d, part]], axis=0)
                add_block(total2, block, ref.hot_root[which * n_col + d])

        yield from fold_all_gather(links, ring_z, longer, lambda d: every.at[:, d], middle_arrived)
        filler.need(ref.root_source)
        rhs2 = ref.root_rhs.at[b]
        summed2 = total2[:share] + total2[share:]
        for part in range(2):
            source2 = ref.t_root_source[part * n_row + row, b]
            rhs2[x, core, part] = source2 + summed2[part * mshare : (part + 1) * mshare]
        yield from row_gather(rhs2)

        filler.need(ref.root_inverse)
        depth = p2 // n_leaf // n_col
        for part in range(2):
            high, low = split(rhs2[:, :, part].reshape(narrow, depth))
            left[part * narrow : (part + 1) * narrow, :depth] = high
            left[width + part * narrow : width + (part + 1) * narrow, :depth] = low
        root = ref.root_terms.at[b]
        each = p2 // n_row // TILE // n_leaf
        product(
            left,
            ref.h_root_inverse,
            ref.l_root_inverse,
            lambda j: root.at[lax.div(j, each), lax.rem(j, each)],
            depth,
            (n_col, cshare, TILE),
        )
        front, back = pl.ds(0, each // 2), pl.ds(each // 2, each - each // 2)

        def z_first():
            yield from fold_reduce_scatter(
                links,
                ring_z,
                longer,
                lambda d: root.at[:, front, d],
                lambda slot: ref.root_land_az.at[b, slot],
            )
            yield from direct_reduce_scatter(
                links,
                ring_y,
                lambda d: root.at[d, front, col],
                lambda slot: ref.root_land_ay.at[b, slot],
            )

        def y_first():
            yield from ring_reduce_scatter(
                links,
                ring_y,
                longer,
                lambda d: root.at[d, back],
                lambda way, step: ref.root_land_by.at[b, (way + 1) // 2, step],
            )
            yield from fold_reduce_scatter(
                links,
                ring_z,
                -longer,
                lambda d: root.at[leaf, back, d],
                lambda slot: ref.root_land_bz.at[b, slot],
            )

        yield from together(y_first(), z_first())
        final = ref.root_final.at[b]
        final[leaf] = root[leaf, :, col]
        yield from direct_all_gather(links, ring_y, lambda d: final.at[d])
        for d in range(n_leaf):
            for j in range(each):
                columns = slice((d * each + j) * TILE, (d * each + j + 1) * TILE)
                ref.root_out[:, b, :, columns] = final[d, j].reshape(2, mshare, TILE)

    run([chain(b) for b in range(BATCHES)], filler)
    assert links.count <= COPIES
    links.close()


def local(
    n_leaf,
    n_row,
    n_col,
    child_source,
    middle_source,
    root_source,
    child_inverse,
    child_update,
    middle_inverse,
    middle_update,
    root_inverse,
    child_diagmask,
    child_updmask,
    middle_diagmask,
    middle_updmask,
    root_diagmask,
    child_rowmap,
    middle_rowmap,
):
    middle_diagmask = middle_diagmask.swapaxes(1, 2)
    root_diagmask = root_diagmask.T
    given = dict(
        child_source=child_source,
        middle_source=middle_source,
        root_source=root_source,
        child_inverse=child_inverse,
        child_update=child_update,
        middle_inverse=middle_inverse,
        middle_update=middle_update,
        root_inverse=root_inverse,
        child_diagmask=child_diagmask,
        child_updmask=child_updmask,
        middle_diagmask=middle_diagmask,
        middle_updmask=middle_updmask,
        root_diagmask=root_diagmask,
        child_rowmap=child_rowmap,
        middle_rowmap=middle_rowmap,
    )
    nrhs = child_source.shape[2]
    p0 = child_inverse.shape[2] * n_col
    p1 = middle_inverse.shape[1] * n_row
    p2 = root_inverse.shape[0] * n_row
    sizes = (n_leaf, n_row, n_col, p0, p1, p2, nrhs)
    n_x = n_row // 2
    width = nrhs // BATCHES
    share, cshare, mshare = width // n_row, width // n_col, width // 2 // n_col
    groups = width // mshare
    reach_y = n_leaf // 2
    t0, t1, t2 = (p // n_row // TILE for p in (p0, p1, p2))
    scratch = dict(
        v_child_inverse=pltpu.VMEM(child_inverse.shape[-2:], F32),
        h_child_inverse=pltpu.VMEM(child_inverse.shape[-2:], BF16),
        l_child_inverse=pltpu.VMEM(child_inverse.shape[-2:], BF16),
        v_child_update=pltpu.VMEM(child_update.shape[-2:], F32),
        h_child_update=pltpu.VMEM(child_update.shape[-2:], BF16),
        l_child_update=pltpu.VMEM(child_update.shape[-2:], BF16),
        v_middle_inverse=pltpu.VMEM(middle_inverse.shape[-2:], F32),
        h_middle_inverse=pltpu.VMEM(middle_inverse.shape[-2:], BF16),
        l_middle_inverse=pltpu.VMEM(middle_inverse.shape[-2:], BF16),
        v_middle_update=pltpu.VMEM(middle_update.shape[-2:], F32),
        h_middle_update=pltpu.VMEM((2 * middle_update.shape[-2], middle_update.shape[-1]), BF16),
        l_middle_update=pltpu.VMEM((2 * middle_update.shape[-2], middle_update.shape[-1]), BF16),
        masked_update=pltpu.VMEM(middle_update.shape[-2:], F32),
        other_update=pltpu.VMEM(middle_update.shape[-2:], F32),
        v_root_inverse=pltpu.VMEM(root_inverse.shape[-2:], F32),
        h_root_inverse=pltpu.VMEM(root_inverse.shape[-2:], BF16),
        l_root_inverse=pltpu.VMEM(root_inverse.shape[-2:], BF16),
        v_child_source=pltpu.VMEM(child_source.shape[-2:], F32),
        t_child_source=pltpu.VMEM((groups, BATCHES, mshare, child_source.shape[-2]), F32),
        v_middle_source=pltpu.VMEM(middle_source.shape[-2:], F32),
        t_middle_source=pltpu.VMEM((groups, BATCHES, mshare, middle_source.shape[-2]), F32),
        v_root_source=pltpu.VMEM(root_source.shape[-2:], F32),
        t_root_source=pltpu.VMEM((groups, BATCHES, mshare, root_source.shape[-2]), F32),
    )
    d1, d2 = p1 // 2 // n_col, p2 // n_leaf // n_col
    depth = max(p0 // n_col, p0 // n_row, d1, p1 // n_row, d2)
    scratch.update(left=pltpu.VMEM((BATCHES, 2 * width, depth), BF16))
    scratch.update(hot_middle=pltpu.VMEM((2 * n_col, d1, TILE), BF16))
    scratch.update(hot_root=pltpu.VMEM((n_leaf * n_col, d2, TILE), BF16))
    shapes = dict(
        child_terms=(BATCHES, t0, n_col, cshare, TILE),
        child_land=(BATCHES, 7, t0, cshare, TILE),
        child_value=(BATCHES, t0, n_col, cshare, TILE),
        child_lift=(BATCHES, 1, n_x, 2, share, TILE),
        child_twin=(BATCHES, 1, n_x, share, TILE),
        child_lift_land=(BATCHES, 7, share, TILE),
        child_lifts=(BATCHES, 2, n_col, share, TILE),
        middle_total=(BATCHES, 2 * share, d1),
        middle_rhs=(BATCHES, n_x, 2, share, d1),
        middle_terms=(BATCHES, t1, 2, n_col, mshare, TILE),
        middle_land=(BATCHES, 7, t1, 2, mshare, TILE),
        middle_pair=(BATCHES, t1, mshare, TILE),
        middle_value=(BATCHES, t1, n_col, mshare, TILE),
        middle_lift=(BATCHES, 2, n_x, 2, mshare, TILE),
        middle_twin=(BATCHES, 2, n_x, mshare, TILE),
        middle_lift_land=(BATCHES, 3, 2, mshare, TILE),
        middle_lifts=(BATCHES, n_leaf, n_col, 2, mshare, TILE),
        root_total=(BATCHES, 2 * share, d2),
        root_rhs=(BATCHES, n_x, 2, 2, mshare, d2),
        root_terms=(BATCHES, n_leaf, t2 // n_leaf, n_col, cshare, TILE),
        root_final=(BATCHES, n_leaf, t2 // n_leaf, cshare, TILE),
        root_land_az=(BATCHES, 7, n_leaf, t2 // n_leaf // 2, cshare, TILE),
        root_land_ay=(BATCHES, 3, t2 // n_leaf // 2, cshare, TILE),
        root_land_by=(BATCHES, 2, reach_y, t2 // n_leaf // 2, n_col, cshare, TILE),
        root_land_bz=(BATCHES, 7, t2 // n_leaf // 2, cshare, TILE),
    )
    for name, shape in shapes.items():
        scratch[name] = pltpu.VMEM(shape, F32)
    scratch.update(send_sems=pltpu.SemaphoreType.DMA((COPIES,)))
    scratch.update(recv_sems=pltpu.SemaphoreType.DMA((COPIES,)))
    scratch.update(load_sems=pltpu.SemaphoreType.DMA((8,)))
    outs = dict(
        child_out=(2, BATCHES, mshare, t0 * TILE),
        middle_out=(BATCHES, mshare, t1 * TILE),
        root_out=(2, BATCHES, mshare, t2 * TILE),
    )
    vmem = pl.BlockSpec(memory_space=pltpu.VMEM)
    whole = pl.BlockSpec(memory_space=pl.ANY)
    child, middle, root = pl.pallas_call(
        functools.partial(kernel, sizes, tuple(given) + tuple(outs) + tuple(scratch)),
        out_shape=[jax.ShapeDtypeStruct(shape, F32) for shape in outs.values()],
        in_specs=[whole] * 8 + [vmem] * 7,
        out_specs=[vmem] * 3,
        scratch_shapes=list(scratch.values()),
        compiler_params=pltpu.CompilerParams(
            collective_id=0, has_side_effects=True, vmem_limit_bytes=60 * 2**20
        ),
    )(*given.values())
    return (
        child.reshape(1, nrhs // n_col, -1).swapaxes(1, 2),
        middle.reshape(1, nrhs // 2 // n_col, -1).swapaxes(1, 2),
        root.reshape(nrhs // n_col, -1).T,
    )


def solution(mesh):
    placed = (
        P("leaf", "col", None),
        P("leaf", "col", None),
        P(("leaf", "col"), None),
        P("leaf", "row", "col"),
        P("leaf", "col", "row"),
        P("leaf", "row", "col"),
        P("leaf", "col", "row"),
        P("row", ("leaf", "col")),
        P("leaf", "row", "col"),
        P("leaf", "col", "row"),
        P("leaf", "row", "col"),
        P("leaf", "col", "row"),
        P("row", ("leaf", "col")),
        P(),
        P(),
    )
    counts = (mesh.shape["leaf"], mesh.shape["row"], mesh.shape["col"])
    return jax.shard_map(
        functools.partial(local, *counts),
        mesh=mesh,
        in_specs=placed,
        out_specs=(P("leaf", "row", "col"), P("leaf", "row", "col"), P("row", "col")),
        check_vma=False,
    )
```

```python
import functools
from types import SimpleNamespace

import jax
import jax.numpy as jnp
from jax import lax
from jax.experimental import pallas as pl
from jax.experimental.pallas import tpu as pltpu
from jax.sharding import PartitionSpec as P

BLK = 128
BATCHES = 3
COPIES = 320
TILE = 256
MESH = pl.DeviceIdType.MESH
F32 = jnp.float32
BF16 = jnp.bfloat16
NT = (((1,), (1,)), ((), ()))


def run(streams, filler=None):
    live = list(streams)
    while live:
        for stream in list(live):
            if next(stream, StopIteration) is StopIteration:
                live.remove(stream)
        if filler is not None:
            filler.step()


def together(*streams):
    live = list(streams)
    while live:
        for stream in list(live):
            if next(stream, StopIteration) is StopIteration:
                live.remove(stream)
        if live:
            yield


class Filler:
    def __init__(self):
        self.tasks = []

    def add(self, name, pieces):
        self.tasks.append((name, pieces))

    def step(self):
        while self.tasks:
            name, pieces = self.tasks[0]
            if next(pieces, StopIteration) is StopIteration:
                self.tasks.pop(0)
            else:
                return

    def need(self, name):
        while any(task[0] is name for task in self.tasks):
            self.step()


class Links:
    def __init__(self, send_sems, recv_sems):
        self.send_sems = send_sems
        self.recv_sems = recv_sems
        self.count = 0
        self.sent = []

    def send(self, source, landing, target):
        index = self.count
        self.count += 1
        copy = pltpu.make_async_remote_copy(
            src_ref=source,
            dst_ref=landing,
            send_sem=self.send_sems.at[index],
            recv_sem=self.recv_sems.at[index],
            device_id=target,
            device_id_type=MESH,
        )
        copy.start()
        self.sent.append(copy)
        return copy

    def close(self):
        for copy in self.sent:
            copy.wait_send()


class Ring:
    def __init__(self, index, length, device, sense=1):
        self.index = index
        self.length = length
        self.device = device
        self.sense = sense

    def at(self, offset):
        return lax.rem(self.index + self.sense * offset + 2 * self.length, self.length)


def ring_reduce_scatter(links, ring, longer, part, landing):
    far = ring.length // 2
    reach = {longer: far, -longer: far - 1}
    before = {}
    for step in range(far + 1):
        if step > 0:
            yield
        for way in (longer, -longer):
            hops = reach[way] - step
            if hops < 0:
                continue
            term = part(ring.at(way * hops))
            if step > 0:
                before[way].wait_recv()
                term[...] = term[...] + landing(way, step - 1)[...]
            if hops > 0:
                before[way] = links.send(term, landing(way, step), ring.device(ring.at(way)))


def fold_reduce_scatter(links, ring, longer, part, landing):
    before = {}
    opposite = links.send(part(ring.at(4)), landing(6), ring.device(ring.at(2 * longer)))
    for step in range(4):
        if step > 0:
            yield
        for way in (longer, -longer):
            term = part(ring.at(way * (3 - step)))
            if step > 0:
                before[way].wait_recv()
                term[...] = term[...] + landing((way + 1) // 2 * 3 + step - 1)[...]
            if step == 1 and way == longer:
                opposite.wait_recv()
                term[...] = term[...] + landing(6)[...]
            if step < 3:
                before[way] = links.send(
                    term, landing((way + 1) // 2 * 3 + step), ring.device(ring.at(way))
                )


def fold_all_gather(links, ring, longer, part, arrived=None):
    before = {}
    for step in range(4):
        if step > 0:
            yield
        new = [ring.index] if step == 0 else []
        for way in (longer, -longer):
            chunk = ring.at(-way * step)
            if step > 0:
                before[way].wait_recv()
                new.append(chunk)
            if step == 2 and way == longer:
                opposite = links.send(part(chunk), part(chunk), ring.device(ring.at(2 * way)))
            if step < 3:
                before[way] = links.send(part(chunk), part(chunk), ring.device(ring.at(way)))
        if arrived is not None:
            for chunk in new:
                arrived(chunk)
    opposite.wait_recv()
    if arrived is not None:
        arrived(ring.at(4))


def direct_reduce_scatter(links, ring, part, landing):
    copies = []
    for slot, offset in enumerate((2, 1, -1)):
        target = ring.at(offset)
        copies.append(links.send(part(target), landing(slot), ring.device(target)))
    yield
    term = part(ring.index)
    for slot in (1, 2, 0):
        copies[slot].wait_recv()
        term[...] = term[...] + landing(slot)[...]


def direct_all_gather(links, ring, part, arrived=None):
    own = part(ring.index)
    copies = []
    for offset in (2, 1, -1):
        copies.append(links.send(own, own, ring.device(ring.at(offset))))
    if arrived is not None:
        arrived(ring.index)
    yield
    for copy, offset in zip(copies[1:] + copies[:1], (1, -1, 2)):
        copy.wait_recv()
        if arrived is not None:
            arrived(ring.at(-offset))


def split(value):
    high = value.astype(BF16)
    return high, (value - high.astype(F32)).astype(BF16)


def product(left, panel_high, panel_low, out, depth, shape):
    count = left.shape[0] // 2

    def tile(j, carry):
        rows = pl.ds(pl.multiple_of(j * TILE, TILE), TILE)
        both = lax.dot_general(left[:, :depth], panel_high[rows, :], NT, preferred_element_type=F32)
        last = lax.dot_general(
            left[:count, :depth], panel_low[rows, :], NT, preferred_element_type=F32
        )
        out(j)[...] = (both[:count] + both[count:] + last).reshape(shape)
        return carry

    lax.fori_loop(0, panel_high.shape[0] // TILE, tile, 0)


def kernel(sizes, names, *refs):
    ref = SimpleNamespace(**dict(zip(names, refs)))
    n_leaf, n_row, n_col, p0, p1, p2, nrhs = sizes
    n_x = n_row // 2
    leaf, row, col = lax.axis_index("leaf"), lax.axis_index("row"), lax.axis_index("col")
    half, couple = lax.rem(leaf, 2), lax.div(leaf, 2)
    x, core = lax.div(row, 2), lax.rem(row, 2)
    ring_y = Ring(leaf, n_leaf, lambda i: {"leaf": i}, 1 - 2 * core)
    ring_z = Ring(col, n_col, lambda i: {"col": i}, 1 - 2 * core)
    ring_x = Ring(x, n_x, lambda i: {"row": i * 2 + core})
    pair = {"leaf": couple * 2 + 1 - half}
    twin = {"row": x * 2 + 1 - core}
    links = Links(ref.send_sems, ref.recv_sems)
    width = nrhs // BATCHES
    share, cshare, mshare = width // n_row, width // n_col, width // 2 // n_col
    groups = width // mshare

    loads = {}
    for index, (source, landing) in enumerate(
        (
            (ref.child_source.at[0], ref.v_child_source),
            (ref.child_inverse.at[0], ref.v_child_inverse),
            (ref.child_update.at[0], ref.v_child_update),
            (ref.middle_source.at[0], ref.v_middle_source),
            (ref.middle_inverse.at[0], ref.v_middle_inverse),
            (ref.middle_update.at[0], ref.v_middle_update),
            (ref.root_source, ref.v_root_source),
            (ref.root_inverse, ref.v_root_inverse),
        )
    ):
        loads[id(landing)] = pltpu.make_async_copy(source, landing, ref.load_sems.at[index])
        if index < 2:
            loads[id(landing)].start()

    barrier = pltpu.get_barrier_semaphore()
    friends = [twin]
    for ring, offsets in ((ring_x, (1, -1, 2)), (ring_y, (1, -1, 2)), (ring_z, (1, -1, 2, -2))):
        friends += [ring.device(ring.at(offset)) for offset in offsets]
    friends += [pair | ring_x.device(ring_x.at(offset)) for offset in (1, -1, 2)]
    for friend in friends:
        pl.semaphore_signal(barrier, inc=1, device_id=friend, device_id_type=MESH)

    def prepare(panel, high, low, mask, first_row, first_col, pieces, masked=None, unrolled=False):
        blocks, across = panel.shape[0] // BLK, panel.shape[1] // BLK
        loads[id(panel)].wait()

        def body(i, carry):
            rows = pl.ds(i * BLK if unrolled else pl.multiple_of(i * BLK, BLK), BLK)
            for j in range(across):
                kept = (mask(i, j) == 1).astype(F32)
                if first_row is not None:
                    down, right = first_row + i, first_col + j
                    kept = jnp.where(down == right, 1.0, jnp.where(down > right, kept, 0.0))
                columns = slice(j * BLK, (j + 1) * BLK)
                block = panel[rows, columns] * kept
                if masked is not None:
                    masked[rows, columns] = block
                top, rest = split(block)
                high[rows, columns] = top
                low[rows, columns] = rest
            return carry

        for piece in range(pieces):
            if unrolled:
                for i in range(blocks * piece // pieces, blocks * (piece + 1) // pieces):
                    body(i, 0)
            else:
                lax.fori_loop(blocks * piece // pieces, blocks * (piece + 1) // pieces, body, 0)
            yield

    def flip(source, flipped):
        loads[id(source)].wait()
        for part in range(source.shape[0] // 256):
            rows = slice(part * 256, (part + 1) * 256)
            flipped[:, :, :, rows] = source[rows, :].T.reshape(groups, BATCHES, mshare, 256)
            yield

    def one_hot(out, rowmap, first, pieces):
        count = out.shape[0]
        place = lax.broadcasted_iota(jnp.int32, out.shape[1:], 0) + first

        def body(k, carry):
            out[k] = (rowmap(k) == place).astype(F32).astype(BF16)
            return carry

        for piece in range(pieces):
            lax.fori_loop(count * piece // pieces, count * (piece + 1) // pieces, body, 0)
            yield

    def child_map(k):
        columns = pl.ds(pl.multiple_of(lax.rem(k, n_col) * TILE, TILE), TILE)
        return ref.child_rowmap[pl.ds(2 * couple + lax.div(k, n_col), 1), columns]

    def middle_map(k):
        owner = lax.div(k, n_col)
        start = (lax.rem(owner, 2) * n_col + lax.rem(k, n_col)) * TILE
        columns = pl.ds(pl.multiple_of(start, TILE), TILE)
        return ref.middle_rowmap[pl.ds(lax.div(owner, 2), 1), columns]

    middle_first = (half * n_col + col) * (p1 // 2 // n_col)
    root_first = (leaf * n_col + col) * (p2 // n_leaf // n_col)
    rows1 = p1 // 4 // n_col
    swap = []

    def share_update():
        here = pl.ds(pl.multiple_of(half * rows1, rows1), rows1)
        yield from prepare(
            ref.v_middle_update,
            ref.h_middle_update.at[here],
            ref.l_middle_update.at[here],
            lambda i, j: ref.middle_updmask[0, pl.ds(i, 1), j : j + 1],
            None,
            None,
            2,
            ref.masked_update,
        )
        swap.append(links.send(ref.masked_update, ref.other_update, pair))

    def split_other():
        swap[0].wait_recv()
        for start in range(0, rows1, BLK):
            there = pl.ds(pl.multiple_of((1 - half) * rows1 + start, BLK), BLK)
            top, rest = split(ref.other_update[start : start + BLK, :])
            ref.h_middle_update[there, :] = top
            ref.l_middle_update[there, :] = rest
            yield

    filler = Filler()
    filler.add(ref.masked_update, share_update())
    filler.add(ref.child_update,
        prepare(ref.v_child_update, ref.h_child_update, ref.l_child_update, lambda i, j: ref.child_updmask[0, pl.ds(i, 1), j : j + 1], None, None, 1),
    )
    filler.add(ref.hot_middle, one_hot(ref.hot_middle, child_map, middle_first, 4))
    filler.add(ref.middle_source, flip(ref.v_middle_source, ref.t_middle_source))
    filler.add(ref.middle_inverse,
        prepare(ref.v_middle_inverse, ref.h_middle_inverse, ref.l_middle_inverse,
            lambda i, j: ref.middle_diagmask[0, j : j + 1, i : i + 1],
            row * (p1 // n_row // BLK),
            lax.div(middle_first, BLK),
            4,
            unrolled=True,
        ),
    )
    filler.add(ref.middle_update, split_other())
    filler.add(ref.root_source, flip(ref.v_root_source, ref.t_root_source))
    filler.add(ref.hot_root, one_hot(ref.hot_root, middle_map, root_first, 8))
    filler.add(ref.root_inverse,
        prepare(ref.v_root_inverse, ref.h_root_inverse, ref.l_root_inverse,
            lambda i, j: ref.root_diagmask[j : j + 1, i : i + 1],
            row * (p2 // n_row // BLK),
            lax.div(root_first, BLK),
            8,
            unrolled=True,
        ),
    )

    for _ in prepare(ref.v_child_inverse, ref.h_child_inverse, ref.l_child_inverse,
        lambda i, j: ref.child_diagmask[0, pl.ds(i, 1), j : j + 1],
        row * (p0 // n_row // BLK),
        col * (p0 // n_col // BLK),
        1,
    ):
        pass
    for _ in flip(ref.v_child_source, ref.t_child_source):
        pass
    for load in list(loads.values())[2:]:
        load.start()

    def chain(b):
        longer = 1 if b == 1 else -1
        left = ref.left.at[b]

        def fill_left(value, columns):
            high, low = split(value)
            left[:width, columns] = high
            left[width:, columns] = low

        def lift_reduce(lift, twin_land, land):
            copy = links.send(lift.at[:, :, 1 - core], twin_land, twin)
            yield
            copy.wait_recv()
            lift[:, :, core] = lift[:, :, core] + twin_land[...]
            yield from direct_reduce_scatter(
                links, ring_x, lambda d: lift.at[:, d, core], lambda slot: land.at[slot]
            )

        def row_gather(buffer):
            copies = []

            def arrived(d):
                copies.append(links.send(buffer.at[d, core], buffer.at[d, core], twin))

            yield from direct_all_gather(links, ring_x, lambda d: buffer.at[d, core], arrived)
            yield
            for copy in copies:
                copy.wait_recv()

        def add_block(total, block, hot):
            high = block.astype(BF16).astype(F32)
            both = jnp.concatenate([high, block - high], axis=0).astype(BF16)
            total[...] += lax.dot_general(both, hot, NT, preferred_element_type=F32)

        depth = p0 // n_col
        fill_left(ref.t_child_source[:, b].reshape(width, depth), slice(0, depth))
        terms = ref.child_terms.at[b]
        product(
            left,
            ref.h_child_inverse,
            ref.l_child_inverse,
            lambda j: terms.at[j],
            depth,
            (n_col, cshare, TILE),
        )
        if b == 0:
            pl.semaphore_wait(barrier, len(friends))
        yield from fold_reduce_scatter(
            links, ring_z, longer, lambda d: terms.at[:, d], lambda slot: ref.child_land.at[b, slot]
        )
        value = ref.child_value.at[b]
        value[:, col] = terms[:, col]
        for j in range(p0 // n_row // TILE):
            ref.child_out[:, b, :, j * TILE : (j + 1) * TILE] = terms[j, col].reshape(2, mshare, TILE)
        yield from fold_all_gather(links, ring_z, longer, lambda d: value.at[:, d])

        filler.need(ref.child_update)
        for j in range(p0 // n_row // TILE):
            fill_left(value[j].reshape(width, TILE), slice(j * TILE, (j + 1) * TILE))
        lift = ref.child_lift.at[b]
        product(
            left,
            ref.h_child_update,
            ref.l_child_update,
            lambda j: lift.at[j],
            p0 // n_row,
            (n_x, 2, share, TILE),
        )
        copy = links.send(lift.at[:, :, 1 - core], ref.child_twin.at[b], twin)
        yield
        copy.wait_recv()
        lift[:, :, core] = lift[:, :, core] + ref.child_twin[b]

        land = ref.child_lift_land.at[b]
        copies = []
        for slot, offset in enumerate((2, 1, -1)):
            there = ring_x.at(offset)
            term = lift.at[0, there, core]
            copies.append(links.send(term, land.at[slot], ring_x.device(there)))
            copies.append(links.send(term, land.at[slot + 3], pair | ring_x.device(there)))
        copies.append(links.send(lift.at[0, x, core], land.at[6], pair))
        got = ref.child_lifts.at[b]
        filler.need(ref.hot_middle)
        total = ref.middle_total.at[b]
        total[...] = jnp.zeros_like(total)
        yield
        for copy in copies:
            copy.wait_recv()
        got[half, col] = lift[0, x, core] + land[0] + land[1] + land[2]
        got[1 - half, col] = land[3] + land[4] + land[5] + land[6]

        def child_arrived(d):
            for which in range(2):
                add_block(total, got[which, d], ref.hot_middle[which * n_col + d])

        yield from fold_all_gather(links, ring_z, longer, lambda d: got.at[:, d], child_arrived)
        filler.need(ref.middle_source)
        rhs = ref.middle_rhs.at[b]
        source = ref.t_middle_source[pl.ds(2 * row, 2), b].reshape(share, -1)
        rhs[x, core] = source + total[:share] + total[share:]
        yield from row_gather(rhs)

        filler.need(ref.middle_inverse)
        depth = p1 // 2 // n_col
        fill_left(rhs[...].reshape(width, depth), slice(0, depth))
        mid = ref.middle_terms.at[b]
        tiles = p1 // n_row // TILE
        product(
            left,
            ref.h_middle_inverse,
            ref.l_middle_inverse,
            lambda j: mid.at[j],
            depth,
            (2, n_col, mshare, TILE),
        )
        yield from fold_reduce_scatter(
            links, ring_z, longer, lambda d: mid.at[:, :, d], lambda slot: ref.middle_land.at[b, slot]
        )
        copy = links.send(mid.at[:, 1 - half, col], ref.middle_pair.at[b], pair)
        yield
        copy.wait_recv()
        solved = ref.middle_value.at[b]
        summed = mid[:, half, col] + ref.middle_pair[b]
        solved[:, col] = summed
        for j in range(tiles):
            ref.middle_out[b, :, j * TILE : (j + 1) * TILE] = summed[j]
        yield from fold_all_gather(links, ring_z, longer, lambda d: solved.at[:, d])

        filler.need(ref.middle_update)
        narrow = width // 2
        for j in range(tiles):
            high, low = split(solved[j].reshape(narrow, TILE))
            left[:narrow, j * TILE : (j + 1) * TILE] = high
            left[narrow:width, j * TILE : (j + 1) * TILE] = low
        lift2 = ref.middle_lift.at[b]
        product(
            left.at[:width],
            ref.h_middle_update,
            ref.l_middle_update,
            lambda j: lift2.at[j],
            p1 // n_row,
            (n_x, 2, mshare, TILE),
        )
        yield from lift_reduce(lift2, ref.middle_twin.at[b], ref.middle_lift_land.at[b])

        every = ref.middle_lifts.at[b]
        every[leaf, col] = lift2[:, x, core]
        yield from direct_all_gather(links, ring_y, lambda d: every.at[d, col])
        filler.need(ref.hot_root)
        total2 = ref.root_total.at[b]
        total2[...] = jnp.zeros_like(total2)

        def middle_arrived(d):
            for which in range(n_leaf):
                first, part = which // 2 * 2, which % 2
                block = jnp.concatenate([every[first, d, part], every[first + 1, d, part]], axis=0)
                add_block(total2, block, ref.hot_root[which * n_col + d])

        yield from fold_all_gather(links, ring_z, longer, lambda d: every.at[:, d], middle_arrived)
        filler.need(ref.root_source)
        rhs2 = ref.root_rhs.at[b]
        summed2 = total2[:share] + total2[share:]
        for part in range(2):
            source2 = ref.t_root_source[part * n_row + row, b]
            rhs2[x, core, part] = source2 + summed2[part * mshare : (part + 1) * mshare]
        yield from row_gather(rhs2)

        filler.need(ref.root_inverse)
        depth = p2 // n_leaf // n_col
        for part in range(2):
            high, low = split(rhs2[:, :, part].reshape(narrow, depth))
            left[part * narrow : (part + 1) * narrow, :depth] = high
            left[width + part * narrow : width + (part + 1) * narrow, :depth] = low
        root = ref.root_terms.at[b]
        each = p2 // n_row // TILE // n_leaf
        product(
            left,
            ref.h_root_inverse,
            ref.l_root_inverse,
            lambda j: root.at[lax.div(j, each), lax.rem(j, each)],
            depth,
            (n_col, cshare, TILE),
        )
        front, back = pl.ds(0, each // 2), pl.ds(each // 2, each - each // 2)

        def z_first():
            yield from fold_reduce_scatter(
                links,
                ring_z,
                longer,
                lambda d: root.at[:, front, d],
                lambda slot: ref.root_land_az.at[b, slot],
            )
            yield from direct_reduce_scatter(
                links,
                ring_y,
                lambda d: root.at[d, front, col],
                lambda slot: ref.root_land_ay.at[b, slot],
            )

        def y_first():
            yield from ring_reduce_scatter(
                links,
                ring_y,
                longer,
                lambda d: root.at[d, back],
                lambda way, step: ref.root_land_by.at[b, (way + 1) // 2, step],
            )
            yield from fold_reduce_scatter(
                links,
                ring_z,
                -longer,
                lambda d: root.at[leaf, back, d],
                lambda slot: ref.root_land_bz.at[b, slot],
            )

        yield from together(y_first(), z_first())
        final = ref.root_final.at[b]
        final[leaf] = root[leaf, :, col]
        yield from direct_all_gather(links, ring_y, lambda d: final.at[d])
        for d in range(n_leaf):
            for j in range(each):
                columns = slice((d * each + j) * TILE, (d * each + j + 1) * TILE)
                ref.root_out[:, b, :, columns] = final[d, j].reshape(2, mshare, TILE)

    run([chain(b) for b in range(BATCHES)], filler)
    assert links.count <= COPIES
    links.close()


def local(
    n_leaf,
    n_row,
    n_col,
    child_source,
    middle_source,
    root_source,
    child_inverse,
    child_update,
    middle_inverse,
    middle_update,
    root_inverse,
    child_diagmask,
    child_updmask,
    middle_diagmask,
    middle_updmask,
    root_diagmask,
    child_rowmap,
    middle_rowmap,
):
    middle_diagmask = middle_diagmask.swapaxes(1, 2)
    root_diagmask = root_diagmask.T
    given = dict(
        child_source=child_source,
        middle_source=middle_source,
        root_source=root_source,
        child_inverse=child_inverse,
        child_update=child_update,
        middle_inverse=middle_inverse,
        middle_update=middle_update,
        root_inverse=root_inverse,
        child_diagmask=child_diagmask,
        child_updmask=child_updmask,
        middle_diagmask=middle_diagmask,
        middle_updmask=middle_updmask,
        root_diagmask=root_diagmask,
        child_rowmap=child_rowmap,
        middle_rowmap=middle_rowmap,
    )
    nrhs = child_source.shape[2]
    p0 = child_inverse.shape[2] * n_col
    p1 = middle_inverse.shape[1] * n_row
    p2 = root_inverse.shape[0] * n_row
    sizes = (n_leaf, n_row, n_col, p0, p1, p2, nrhs)
    n_x = n_row // 2
    width = nrhs // BATCHES
    share, cshare, mshare = width // n_row, width // n_col, width // 2 // n_col
    groups = width // mshare
    reach_y = n_leaf // 2
    t0, t1, t2 = (p // n_row // TILE for p in (p0, p1, p2))
    scratch = dict(
        v_child_inverse=pltpu.VMEM(child_inverse.shape[-2:], F32),
        h_child_inverse=pltpu.VMEM(child_inverse.shape[-2:], BF16),
        l_child_inverse=pltpu.VMEM(child_inverse.shape[-2:], BF16),
        v_child_update=pltpu.VMEM(child_update.shape[-2:], F32),
        h_child_update=pltpu.VMEM(child_update.shape[-2:], BF16),
        l_child_update=pltpu.VMEM(child_update.shape[-2:], BF16),
        v_middle_inverse=pltpu.VMEM(middle_inverse.shape[-2:], F32),
        h_middle_inverse=pltpu.VMEM(middle_inverse.shape[-2:], BF16),
        l_middle_inverse=pltpu.VMEM(middle_inverse.shape[-2:], BF16),
        v_middle_update=pltpu.VMEM(middle_update.shape[-2:], F32),
        h_middle_update=pltpu.VMEM((2 * middle_update.shape[-2], middle_update.shape[-1]), BF16),
        l_middle_update=pltpu.VMEM((2 * middle_update.shape[-2], middle_update.shape[-1]), BF16),
        masked_update=pltpu.VMEM(middle_update.shape[-2:], F32),
        other_update=pltpu.VMEM(middle_update.shape[-2:], F32),
        v_root_inverse=pltpu.VMEM(root_inverse.shape[-2:], F32),
        h_root_inverse=pltpu.VMEM(root_inverse.shape[-2:], BF16),
        l_root_inverse=pltpu.VMEM(root_inverse.shape[-2:], BF16),
        v_child_source=pltpu.VMEM(child_source.shape[-2:], F32),
        t_child_source=pltpu.VMEM((groups, BATCHES, mshare, child_source.shape[-2]), F32),
        v_middle_source=pltpu.VMEM(middle_source.shape[-2:], F32),
        t_middle_source=pltpu.VMEM((groups, BATCHES, mshare, middle_source.shape[-2]), F32),
        v_root_source=pltpu.VMEM(root_source.shape[-2:], F32),
        t_root_source=pltpu.VMEM((groups, BATCHES, mshare, root_source.shape[-2]), F32),
    )
    d1, d2 = p1 // 2 // n_col, p2 // n_leaf // n_col
    depth = max(p0 // n_col, p0 // n_row, d1, p1 // n_row, d2)
    scratch.update(left=pltpu.VMEM((BATCHES, 2 * width, depth), BF16))
    scratch.update(hot_middle=pltpu.VMEM((2 * n_col, d1, TILE), BF16))
    scratch.update(hot_root=pltpu.VMEM((n_leaf * n_col, d2, TILE), BF16))
    shapes = dict(
        child_terms=(BATCHES, t0, n_col, cshare, TILE),
        child_land=(BATCHES, 7, t0, cshare, TILE),
        child_value=(BATCHES, t0, n_col, cshare, TILE),
        child_lift=(BATCHES, 1, n_x, 2, share, TILE),
        child_twin=(BATCHES, 1, n_x, share, TILE),
        child_lift_land=(BATCHES, 7, share, TILE),
        child_lifts=(BATCHES, 2, n_col, share, TILE),
        middle_total=(BATCHES, 2 * share, d1),
        middle_rhs=(BATCHES, n_x, 2, share, d1),
        middle_terms=(BATCHES, t1, 2, n_col, mshare, TILE),
        middle_land=(BATCHES, 7, t1, 2, mshare, TILE),
        middle_pair=(BATCHES, t1, mshare, TILE),
        middle_value=(BATCHES, t1, n_col, mshare, TILE),
        middle_lift=(BATCHES, 2, n_x, 2, mshare, TILE),
        middle_twin=(BATCHES, 2, n_x, mshare, TILE),
        middle_lift_land=(BATCHES, 3, 2, mshare, TILE),
        middle_lifts=(BATCHES, n_leaf, n_col, 2, mshare, TILE),
        root_total=(BATCHES, 2 * share, d2),
        root_rhs=(BATCHES, n_x, 2, 2, mshare, d2),
        root_terms=(BATCHES, n_leaf, t2 // n_leaf, n_col, cshare, TILE),
        root_final=(BATCHES, n_leaf, t2 // n_leaf, cshare, TILE),
        root_land_az=(BATCHES, 7, n_leaf, t2 // n_leaf // 2, cshare, TILE),
        root_land_ay=(BATCHES, 3, t2 // n_leaf // 2, cshare, TILE),
        root_land_by=(BATCHES, 2, reach_y, t2 // n_leaf // 2, n_col, cshare, TILE),
        root_land_bz=(BATCHES, 7, t2 // n_leaf // 2, cshare, TILE),
    )
    for name, shape in shapes.items():
        scratch[name] = pltpu.VMEM(shape, F32)
    scratch.update(send_sems=pltpu.SemaphoreType.DMA((COPIES,)))
    scratch.update(recv_sems=pltpu.SemaphoreType.DMA((COPIES,)))
    scratch.update(load_sems=pltpu.SemaphoreType.DMA((8,)))
    outs = dict(
        child_out=(2, BATCHES, mshare, t0 * TILE),
        middle_out=(BATCHES, mshare, t1 * TILE),
        root_out=(2, BATCHES, mshare, t2 * TILE),
    )
    vmem = pl.BlockSpec(memory_space=pltpu.VMEM)
    whole = pl.BlockSpec(memory_space=pl.ANY)
    child, middle, root = pl.pallas_call(
        functools.partial(kernel, sizes, tuple(given) + tuple(outs) + tuple(scratch)),
        out_shape=[jax.ShapeDtypeStruct(shape, F32) for shape in outs.values()],
        in_specs=[whole] * 8 + [vmem] * 7,
        out_specs=[vmem] * 3,
        scratch_shapes=list(scratch.values()),
        compiler_params=pltpu.CompilerParams(
            collective_id=0, has_side_effects=True, vmem_limit_bytes=60 * 2**20
        ),
    )(*given.values())
    return (
        child.reshape(1, nrhs // n_col, -1).swapaxes(1, 2),
        middle.reshape(1, nrhs // 2 // n_col, -1).swapaxes(1, 2),
        root.reshape(nrhs // n_col, -1).T,
    )


def solution(mesh):
    placed = (
        P("leaf", "col", None),
        P("leaf", "col", None),
        P(("leaf", "col"), None),
        P("leaf", "row", "col"),
        P("leaf", "col", "row"),
        P("leaf", "row", "col"),
        P("leaf", "col", "row"),
        P("row", ("leaf", "col")),
        P("leaf", "row", "col"),
        P("leaf", "col", "row"),
        P("leaf", "row", "col"),
        P("leaf", "col", "row"),
        P("row", ("leaf", "col")),
        P(),
        P(),
    )
    counts = (mesh.shape["leaf"], mesh.shape["row"], mesh.shape["col"])
    return jax.shard_map(
        functools.partial(local, *counts),
        mesh=mesh,
        in_specs=placed,
        out_specs=(P("leaf", "row", "col"), P("leaf", "row", "col"), P("row", "col")),
        check_vma=False,
    )
```
